512 devices in a mesh: member: 8 (over z_hi, core), grid: 64 (over x, z_lo, y).
Axes of the slice: x: 4, y: 8, z: 8 (z_hi: 4, z_lo: 2; z = z_hi * 2 + z_lo), core: 2. Of those that a mesh axis runs over, the one named last changes fastest.
Arguments:
- mesh_latent: bfloat16 [8, 512, 8192], P('member', None, 'grid'), may hold values from -6 to 6
- grid_latent: bfloat16 [8, 512, 65536], P('member', None, 'grid'), may hold values from -6 to 6
- edge_sources: int32 [3, 65536], P(None, 'grid'), may hold values from 0 to 8191, as said below
- edge_weights: bfloat16 [3, 65536], P(None, 'grid'), may hold values from 0.19921875 to 1
- area_weight: float32 [65536], P('grid'), may hold values from 0.3 to 1.7
- band_counts: int32 [64], P('grid'), may hold values from 256 to 1024, as said below
- target: bfloat16 [100, 65536], P(None, 'grid'), may hold values from -3 to 3
- hidden_weight: bfloat16 [512, 512], replicated, may hold values from -0.25 to 0.25
- out_weight: bfloat16 [512, 100], replicated, may hold values from -0.25 to 0.25
Outputs:
- grad_hidden_weight: float32 [512, 512], P('grid')
- grad_out_weight: float32 [512, 100], P('grid')
- grad_mesh: float32 [8, 512, 8192], P('member', None, 'grid')
The draws below stay inside these ranges and needn't reach their ends.
Inputs may be any that keep to these rules, and one draw needn't show every extreme that they name: `edge_sources`: the 3 nodes of one grid point are distinct and lie in its own band's nodes or within 64 nodes on either side of them; band b holds nodes b * 128 to (b + 1) * 128 - 1 and grid slots b * 1024 to (b + 1) * 1024 - 1. `band_counts`: some band is full.
All inputs are finite; a program needn't handle non-finite values.
Results may differ from the reference program's by a relative error of at most 0.04.
Values may be sent and summed in bfloat16 or wider, within the bound.
A program may use at most 64 MiB of HBM per device.

```python
import jax
import jax.numpy as jnp
from jax import lax

D = 512
V = 100
P_DEV = 1024
NODE_DEV = 128
HALO = 64
EDGES = 3
MEMBERS = 8
BANDS = 64
POINTS = 65536
NODES = 8192


def draw_edge_sources(key, part):
    key = jax.random.fold_in(key, 11)
    first_key, second_key = jax.random.split(key)
    band = jnp.arange(POINTS, dtype=jnp.int32) // P_DEV
    lower = jnp.maximum(band * NODE_DEV - HALO, 0)
    upper = jnp.minimum((band + 1) * NODE_DEV + HALO, NODES)
    span = upper - lower
    base = jax.random.randint(first_key, (POINTS,), 0, span)
    stride = jax.random.randint(second_key, (POINTS,), 1, span // EDGES + 1)
    offsets = (base[None, :] + jnp.arange(EDGES, dtype=jnp.int32)[:, None] * stride[None, :]) % span[None, :]
    return (lower[None, :] + offsets).astype(jnp.int32)


def draw_band_counts(key, part):
    key = jax.random.fold_in(key, 7)
    first_key, second_key = jax.random.split(key)
    counts = jax.random.randint(first_key, (BANDS,), P_DEV // 4, P_DEV + 1)
    full_band = jax.random.randint(second_key, (), 0, BANDS)
    counts = jnp.where(jnp.arange(BANDS, dtype=jnp.int32) == full_band, P_DEV, counts)
    return counts.astype(jnp.int32)


def block_levels(own_key, shape, pieces, low, largest):
    loudness, own = 1.0, jax.random.fold_in(own_key, 6)
    for dim, blocks in pieces:
        steps = jnp.exp(jax.random.uniform(jax.random.fold_in(own, dim), (blocks,), jnp.float32, low / len(pieces), largest / len(pieces)))
        loudness = loudness * jnp.repeat(steps, shape[dim] // blocks).reshape([-1 if axis == dim else 1 for axis in range(len(shape))])
    return loudness


def scatter_about(own_key, extent, spread, most, cuts=(), kind=jnp.bfloat16):
    values = jax.random.normal(own_key, extent, jnp.float32) * spread
    if len(cuts) > 0:
        values = block_levels(own_key, extent, cuts, -0.22, 0.18) * values
    return jnp.clip(values, min=-most, max=most).astype(kind)


def setup_inputs(seed: int = 0) -> dict:
    key_of = jax.random.split(jax.random.key(seed), 10)
    return {
        "mesh_latent": scatter_about(key_of[0], (MEMBERS, D, NODES), 1.0, 6.0, ((0, 8), (2, 64))),
        "grid_latent": scatter_about(key_of[1], (MEMBERS, D, POINTS), 1.0, 6.0, ((0, 8), (2, 64))),
        "edge_sources": draw_edge_sources(jax.random.fold_in(key_of[9], 71), 0),
        "edge_weights": jnp.clip(0.19921875 + 0.80078125 * jax.random.uniform(key_of[3], (EDGES, POINTS), jnp.float32) ** block_levels(key_of[3], (EDGES, POINTS), ((1, 64),), -0.2, 0.2), 0.19921875, 1.0).astype(jnp.bfloat16),
        "area_weight": jnp.clip(0.3 + 1.40000004 * jax.random.uniform(key_of[4], (POINTS,), jnp.float32) ** block_levels(key_of[4], (POINTS,), ((0, 64),), -0.2, 0.2), 0.3, 1.7),
        "band_counts": draw_band_counts(jax.random.fold_in(key_of[9], 71), 0),
        "target": scatter_about(key_of[6], (V, POINTS), 0.5, 3.0, ((1, 64),)),
        "hidden_weight": scatter_about(key_of[7], (D, D), D ** -0.5, 0.25),
        "out_weight": scatter_about(key_of[8], (D, V), D ** -0.5, 0.25),
    }


smooth_sq = 0.01
loss_scale = 4096.0

def slope(diff):
    return diff / jnp.sqrt(diff * diff + smooth_sq)

def forward(mesh_one, grid_one, edge_sources, edge_weights, hidden_weight, out_weight):
    agg = jnp.zeros(grid_one.shape, jnp.float32)
    for k in range(EDGES):
        agg = agg + edge_weights[k].astype(jnp.float32)[None, :] * jnp.take(mesh_one, edge_sources[k], axis=1).astype(jnp.float32)
    x_in = (agg + grid_one.astype(jnp.float32)).astype(jnp.bfloat16)
    pre = lax.dot_general(hidden_weight, x_in, (((0,), (0,)), ((), ())), preferred_element_type=jnp.float32)
    sig = jax.nn.sigmoid(pre)
    hidden = (pre * sig).astype(jnp.bfloat16)
    pred = lax.dot_general(out_weight, hidden, (((0,), (0,)), ((), ())), preferred_element_type=jnp.float32).astype(jnp.bfloat16)
    return (x_in, pre, sig, hidden, pred)

def reference(mesh_latent, grid_latent, edge_sources, edge_weights, area_weight, band_counts, target, hidden_weight, out_weight):
    points = jnp.arange(POINTS, dtype=jnp.int32)
    live = (points % P_DEV < band_counts[points // P_DEV]).astype(jnp.float32)
    coef = loss_scale * area_weight * live / V
    preds = []
    for m in range(MEMBERS):
        preds.append(forward(mesh_latent[m], grid_latent[m], edge_sources, edge_weights, hidden_weight, out_weight)[4])
    grad_hidden = jnp.zeros((D, D), jnp.float32)
    grad_out = jnp.zeros((D, V), jnp.float32)
    grad_mesh = []
    target_f = target.astype(jnp.float32)
    for m in range(MEMBERS):
        x_in, pre, sig, hidden, pred = forward(mesh_latent[m], grid_latent[m], edge_sources, edge_weights, hidden_weight, out_weight)
        pred_f = pred.astype(jnp.float32)
        own = slope(pred_f - target_f)
        pair = jnp.zeros(pred_f.shape, jnp.float32)
        for j in range(MEMBERS):
            pair = pair + slope(pred_f - preds[j].astype(jnp.float32))
        gpred = (coef[None, :] * (own / MEMBERS - pair / (MEMBERS * (MEMBERS - 1)))).astype(jnp.bfloat16)
        dh = jnp.dot(out_weight, gpred, preferred_element_type=jnp.float32)
        dpre = (dh * sig * (1.0 + pre * (1.0 - sig))).astype(jnp.bfloat16)
        dx = jnp.dot(hidden_weight, dpre, preferred_element_type=jnp.float32).astype(jnp.bfloat16)
        grad_hidden = grad_hidden + lax.dot_general(x_in, dpre, (((1,), (1,)), ((), ())), preferred_element_type=jnp.float32)
        grad_out = grad_out + lax.dot_general(hidden, gpred, (((1,), (1,)), ((), ())), preferred_element_type=jnp.float32)
        dx_rows = dx.astype(jnp.float32).T
        node_grad = jnp.zeros((NODES, D), jnp.float32)
        for k in range(EDGES):
            node_grad = node_grad + jax.ops.segment_sum(dx_rows * edge_weights[k].astype(jnp.float32)[:, None], edge_sources[k], NODES)
        grad_mesh.append(node_grad.T)
    return (grad_hidden, grad_out, jnp.stack(grad_mesh, axis=0))
```

```python
import functools

import jax
import jax.numpy as jnp
from jax import lax
from jax.experimental import pallas as pl
from jax.experimental.pallas import tpu as pltpu
from jax.sharding import PartitionSpec as P

HALO = 64
LANES = 128
CHUNKS = 2
BLOCKS = 4
ROWS = 48
MAIN = 96
EXTRA = 16
MESH = pl.DeviceIdType.MESH

smooth_sq = 0.01
loss_scale = 4096.0

F32 = jnp.float32
BF16 = jnp.bfloat16


def slope(diff):
    return diff * lax.rsqrt(diff * diff + smooth_sq)


def dot(a, b, da, db):
    return lax.dot_general(a, b, (((da,), (db,)), ((), ())), preferred_element_type=F32)


def low_lanes(shape):
    return lax.broadcasted_iota(jnp.int32, shape, 1) < HALO


def pack(tile):
    half = tile.shape[0] // 2
    top, bottom = tile[:half], tile[half:]
    low = low_lanes(top.shape)
    down = jnp.where(low, top, pltpu.roll(bottom, HALO, 1))
    up = jnp.where(low, pltpu.roll(top, HALO, 1), bottom)
    return down, up


def unpack(below, above):
    low = low_lanes(below.shape)
    top = jnp.where(low, below, pltpu.roll(above, HALO, 1))
    bottom = jnp.where(low, pltpu.roll(below, HALO, 1), above)
    return top, bottom


def kernel(
    dims,
    mesh_in, grid_in, src_in, wgt_in, area_in, count_in, target_in, hw_in, ow_in,
    gh_out, go_out, gm_out,
    mesh_v, grid_v, src_v, wgt_v, area_v, count_v, tgt_v, hw_v, ow_v,
    tgt_f, coef_v, hw_t, ow_f, ow_r, ow_t, ext_v, adj_v, x_v, h_v, f_v,
    halo_s, halo_r, ghalo_s, ghalo_r,
    pred_s, pext_s, pred_r, pext_r, grad_s, gext_s, grad_r, gext_r,
    gw_v, eg_v, s0_s, s0_r, s1_s, s1_r, sum_v, s2_s, s2_r, s3_s, s3_r, gh_v, go_v, gm_v,
    load_sem, store_sem, halo_sem, ghalo_sem, p_sem, pe_send, pe_recv, g_sem, ge_send, ge_recv,
    s0_sem, s1_sem, s2_sem, s3_send, s3_recv,
):
    nx, nl, ny = dims
    nodes = mesh_v.shape[1]
    depth = hw_v.shape[0]
    width = depth + LANES
    points = grid_v.shape[1] // CHUNKS
    member, band = lax.axis_index("member"), lax.axis_index("grid")
    zh, core = member // 2, member % 2
    xi, zl, yi = band // (nl * ny), (band // ny) % nl, band % ny
    bands = nx * nl * ny

    def at(zh_=None, core_=None, x_=None, zl_=None, y_=None):
        zh_ = zh if zh_ is None else zh_
        core_ = core if core_ is None else core_
        x_ = xi if x_ is None else x_
        zl_ = zl if zl_ is None else zl_
        y_ = yi if y_ is None else y_
        return (zh_ * 2 + core_, x_ * (nl * ny) + zl_ * ny + y_)

    above = (member, (band + 1) % bands)
    below = (member, (band + bands - 1) % bands)

    def remote(src, dst, sems, i, device):
        return pltpu.make_async_remote_copy(
            src_ref=src, dst_ref=dst, send_sem=sems.at[0, i], recv_sem=sems.at[1, i],
            device_id=device, device_id_type=MESH,
        )

    barrier = pltpu.get_barrier_semaphore()
    partners = [above, below]
    partners += [at(x_=(xi + s) % nx) for s in range(1, nx)]
    partners += [at(y_=(yi + s) % ny) for s in range(1, ny)]
    partners += [
        at(zh_=(zh + a) % 4, core_=(core + b) % 2, zl_=(zl + c) % nl)
        for a in range(4) for b in range(2) for c in range(nl) if (a, b, c) != (0, 0, 0)
    ]
    for partner in partners:
        pl.semaphore_signal(barrier, inc=1, device_id=partner, device_id_type=MESH)

    def load(i, src, dst):
        copy = pltpu.make_async_copy(src, dst, load_sem.at[i])
        copy.start()
        return copy

    load_mesh = load(0, mesh_in.at[0], mesh_v)
    load_src = load(1, src_in, src_v)
    load_wgt = load(2, wgt_in, wgt_v)
    load_hw = load(3, hw_in, hw_v)
    load_ow = load(4, ow_in, ow_v)
    load_grid = load(5, grid_in.at[0], grid_v)
    load_area = load(6, area_in, area_v)
    load_tgt = load(7, target_in, tgt_v)
    load_count = load(8, count_in, count_v)

    load_mesh.wait()
    down, up = pack(mesh_v[...].astype(F32))
    halo_s[0] = down.astype(BF16)
    halo_s[1] = up.astype(BF16)
    pl.semaphore_wait(barrier, len(partners))
    halo_down = remote(halo_s.at[0], halo_r.at[0], halo_sem, 0, below)
    halo_up = remote(halo_s.at[1], halo_r.at[1], halo_sem, 1, above)
    halo_down.start()
    halo_up.start()

    ext_v[:, 0:nodes] = mesh_v[...]

    load_hw.wait()
    hw_t[...] = hw_v[...].astype(F32).T.astype(BF16)
    load_ow.wait()
    count = ow_v.shape[0]
    ow_f[MAIN:LANES] = jnp.zeros((LANES - MAIN, depth), F32)
    ow_f[0:count] = ow_v[...].astype(F32)
    tail = ow_f[MAIN : MAIN + 8]
    tail = tail + pltpu.roll(tail, 4, 0)
    ow_f[MAIN : MAIN + 8] = tail
    ow_f[MAIN + 8 : MAIN + 16] = tail
    ow_t[...] = ow_f[...].astype(BF16)
    ow_r[...] = ow_f[...].T.astype(BF16)

    load_src.wait()
    load_wgt.wait()
    row = lax.broadcasted_iota(jnp.int32, (nodes + 2 * HALO, points), 0)
    slot = jnp.where(row < nodes, row, jnp.where(row < nodes + HALO, row - (nodes + HALO), row - HALO))
    for chunk in range(CHUNKS):
        cols = pl.ds(chunk * points, points)
        adj = jnp.zeros(row.shape, F32)
        for k in range(3):
            source = src_v[pl.ds(k, 1), cols] - band * nodes
            weight = wgt_v[:, cols].astype(F32)[k : k + 1]
            adj = jnp.where(source == slot, weight, adj)
        adj_v[:, cols] = adj.astype(BF16)

    load_tgt.wait()
    tgt_f[0 : tgt_v.shape[0]] = tgt_v[...].astype(F32)
    load_area.wait()
    load_count.wait()
    place = lax.broadcasted_iota(jnp.int32, (1, CHUNKS * points), 1)
    live = (place < count_v[0]).astype(F32)
    coef_v[...] = loss_scale * area_v[...] * live / tgt_v.shape[0]
    group = lax.broadcasted_iota(jnp.int32, (EXTRA, LANES), 0) // 4

    def spread(blocks):
        out = blocks[0]
        for b in range(1, BLOCKS):
            out = jnp.where(group == b, blocks[b], out)
        return out

    load_grid.wait()
    halo_down.wait_recv()
    halo_up.wait_recv()
    top, bottom = unpack(halo_r[1].astype(F32), halo_r[0].astype(F32))
    ext_v[0 : depth // 2, nodes : nodes + 2 * HALO] = top.astype(BF16)
    ext_v[depth // 2 : depth, nodes : nodes + 2 * HALO] = bottom.astype(BF16)

    keepers = (0, 5)
    others = [(a, b) for a in (2, 1, 3, 0) for b in range(2) if (a, b) != (0, 0)]
    sent = []

    def group_device(j):
        return (j, band)

    def my_rows(ref, core_):
        return ref.at[pl.ds(pl.multiple_of(ROWS * core_, 16), ROWS)]

    def forward(chunk):
        cols = pl.ds(chunk * points, points)
        agg = dot(ext_v[...], adj_v[:, cols], 1, 0)
        x_v[:, cols] = (agg + grid_v[:, cols].astype(F32)).astype(BF16)
        pre = dot(hw_t[...], x_v[:, cols], 1, 0)
        sig = 0.5 * jnp.tanh(0.5 * pre) + 0.5
        h_v[:, cols] = (pre * sig).astype(BF16)
        f_v[:, cols] = sig * (1.0 + pre * (1.0 - sig))
        pred = dot(ow_t[...], h_v[:, cols], 1, 0)
        tails = []
        for b in range(BLOCKS):
            block = pred[:, b * LANES : (b + 1) * LANES]
            pred_s[chunk, b] = block[:MAIN].astype(BF16)
            tails.append(block[MAIN : MAIN + EXTRA])
        pext_s[chunk] = spread(tails).astype(BF16)
        copies = []
        for i, (a, b) in enumerate(others):
            z_, c_ = (zh + a) % 4, (core + b) % 2
            copy = remote(my_rows(pred_s.at[chunk, z_], c_), pred_r.at[chunk, member], p_sem, chunk * 7 + i, at(zh_=z_, core_=c_))
            copy.start()
            copies.append(copy)
        keeper = keepers[chunk]

        @pl.when(member != keeper)
        def _():
            pext_copy(chunk).start()

        pred_r[chunk, member] = my_rows(pred_s.at[chunk, zh], core)[...]
        return copies

    def pext_copy(chunk):
        return pltpu.make_async_remote_copy(
            src_ref=pext_s.at[chunk], dst_ref=pext_r.at[chunk, member],
            send_sem=pe_send.at[chunk], recv_sem=pe_recv.at[chunk, member],
            device_id=group_device(keepers[chunk]), device_id_type=MESH,
        )

    def pext_arrival(chunk, j):
        return pltpu.make_async_remote_copy(
            src_ref=pext_s.at[chunk], dst_ref=pext_r.at[chunk, j],
            send_sem=pe_send.at[chunk], recv_sem=pe_recv.at[chunk, j],
            device_id=group_device(j), device_id_type=MESH,
        )

    def gext_copy(chunk, j):
        return pltpu.make_async_remote_copy(
            src_ref=gext_s.at[chunk, j], dst_ref=gext_r.at[chunk],
            send_sem=ge_send.at[chunk, j], recv_sem=ge_recv.at[chunk],
            device_id=group_device(j), device_id_type=MESH,
        )

    def fair(preds, target, weight):
        out = [slope(p - target) * (1.0 / 8.0) for p in preds]
        pairs = [jnp.zeros(target.shape, F32) for _ in preds]
        for i in range(8):
            for j in range(i + 1, 8):
                s = slope(preds[i] - preds[j])
                pairs[i] = pairs[i] + s
                pairs[j] = pairs[j] - s
        return [weight * (o - q * (1.0 / 56.0)) for o, q in zip(out, pairs)]

    def pair_up(chunk, copies):
        for copy in copies:
            copy.wait_recv()
        sent.extend(copies)
        lanes = pl.ds(pl.multiple_of(chunk * points + zh * LANES, LANES), LANES)

        def tile(t, _):
            rows = pl.ds(pl.multiple_of(t * 16, 16), 16)
            target = tgt_f[pl.ds(pl.multiple_of(ROWS * core + t * 16, 16), 16), lanes]
            grads = fair([pred_r[chunk, j, rows].astype(F32) for j in range(8)], target, coef_v[:, lanes])
            for j in range(8):
                grad_s[chunk, j, rows] = grads[j].astype(BF16)
            return 0

        lax.fori_loop(0, ROWS // 16, tile, 0)
        gcopies = []
        for i, (a, b) in enumerate(others):
            z_, c_ = (zh + a) % 4, (core + b) % 2
            copy = remote(grad_s.at[chunk, z_ * 2 + c_], my_rows(grad_r.at[chunk, zh], core), g_sem, chunk * 7 + i, at(zh_=z_, core_=c_))
            copy.start()
            gcopies.append(copy)
        my_rows(grad_r.at[chunk, zh], core)[...] = grad_s[chunk, member]
        keeper = keepers[chunk]

        @pl.when(member == keeper)
        def _():
            pext_r[chunk, keeper] = pext_s[chunk]
            for j in range(8):
                if j != keeper:
                    pext_arrival(chunk, j).wait_recv()
            targets, weights = [], []
            row8 = lax.broadcasted_iota(jnp.int32, (8, LANES), 0)
            for b in range(BLOCKS):
                at_b = pl.ds(chunk * points + b * LANES, LANES)
                tail = tgt_f[MAIN : MAIN + 8, at_b]
                tail = jnp.where(row8 < 4, tail, pltpu.roll(tail, 4, 0))
                targets.append(jnp.concatenate([tail, tail], axis=0))
                weights.append(jnp.broadcast_to(coef_v[:, at_b], (EXTRA, LANES)))
            grads = fair([pext_r[chunk, j].astype(F32) for j in range(8)], spread(targets), spread(weights))
            for j in range(8):
                gext_s[chunk, j] = grads[j].astype(BF16)
            for j in range(8):
                if j != keeper:
                    gext_copy(chunk, j).start()
            gext_r[chunk] = gext_s[chunk, keeper]

        return gcopies

    def backward(chunk, gcopies):
        cols = pl.ds(chunk * points, points)
        for copy in gcopies:
            copy.wait_recv()
        sent.extend(gcopies)
        keeper = keepers[chunk]

        @pl.when(member != keeper)
        def _():
            gext_copy(chunk, 0).wait_recv()

        tail = gext_r[chunk].astype(F32)
        blocks = []
        for b in range(BLOCKS):
            mine = jnp.where(group == b, tail, 0.0).astype(BF16)
            blocks.append(jnp.concatenate([grad_r[chunk, b], mine, jnp.zeros((LANES - MAIN - EXTRA, LANES), BF16)], axis=0))
        gpred = jnp.concatenate(blocks, axis=1)
        dh = dot(ow_r[...], gpred, 1, 0)
        dpre = (dh * f_v[:, cols]).astype(BF16)
        first = dot(x_v[:, cols], dpre, 1, 1)
        second = dot(h_v[:, cols], gpred, 1, 1)
        if chunk == 0:
            gw_v[:, 0:depth] = first
            gw_v[:, depth:width] = second
        else:
            gw_v[:, 0:depth] += first
            gw_v[:, depth:width] += second
        return dpre

    def node_sums(chunk, dpre):
        cols = pl.ds(chunk * points, points)
        dx = dot(hw_v[...], dpre, 1, 0).astype(BF16)
        sums = dot(dx, adj_v[:, cols], 1, 1)
        if chunk == 0:
            eg_v[...] = sums
        else:
            eg_v[...] += sums

    copies = [forward(chunk) for chunk in range(CHUNKS)]
    gcopies = [pair_up(chunk, copies[chunk]) for chunk in range(CHUNKS)]
    for chunk in range(CHUNKS - 1):
        node_sums(chunk, backward(chunk, gcopies[chunk]))
    last = backward(CHUNKS - 1, gcopies[CHUNKS - 1])

    per_x, per_z, per_y = depth // nx, depth // (nx * nl), depth // (nx * nl * ny)

    def part(x_, core_):
        return pl.ds(pl.multiple_of(x_ * per_x + core_ * per_z, 8), per_z)

    for x_ in range(nx):
        s0_s[x_] = gw_v[part(x_, 1 - core), :].astype(BF16)
    s0 = remote(s0_s, s0_r, s0_sem, 0, at(core_=1 - core))
    s0.start()
    sent.append(s0)

    node_sums(CHUNKS - 1, last)
    down, up = pack(eg_v[:, nodes : nodes + 2 * HALO])
    ghalo_s[0] = down.astype(BF16)
    ghalo_s[1] = up.astype(BF16)
    ghalo_down = remote(ghalo_s.at[0], ghalo_r.at[0], ghalo_sem, 0, below)
    ghalo_up = remote(ghalo_s.at[1], ghalo_r.at[1], ghalo_sem, 1, above)

    s0.wait_recv()
    for x_ in range(nx):
        s1_s[x_] = (gw_v[part(x_, core), :] + s0_r[x_].astype(F32)).astype(BF16)
    s1 = []
    for s in range(1, nx):
        x_ = (xi + s) % nx
        copy = remote(s1_s.at[x_], s1_r.at[s - 1], s1_sem, s - 1, at(x_=x_))
        copy.start()
        s1.append(copy)
    ghalo_down.start()
    ghalo_up.start()
    total = gw_v[part(xi, core), :] + s0_r[xi].astype(F32)
    for copy in s1:
        copy.wait_recv()
    sent.extend(s1)
    for s in range(nx - 1):
        total = total + s1_r[s].astype(F32)
    half = 3 * LANES
    for y_ in range(ny):
        rows = total[y_ * per_y : (y_ + 1) * per_y]
        rest = jnp.concatenate([rows[:, half:width], jnp.zeros((per_y, 2 * half - width), F32)], axis=1)
        sum_v[y_] = jnp.concatenate([rows[:, 0:half], rest], axis=0)
        s2_s[y_] = sum_v[y_].astype(BF16)
    s2 = []
    for s in range(1, ny):
        y_ = (yi + s) % ny
        copy = remote(s2_s.at[y_], s2_r.at[s - 1], s2_sem, s - 1, at(y_=y_))
        copy.start()
        s2.append(copy)

    ghalo_down.wait_recv()
    ghalo_up.wait_recv()
    sent.extend([ghalo_down, ghalo_up])
    top, bottom = unpack(ghalo_r[1].astype(F32), ghalo_r[0].astype(F32))
    gm_v[0 : depth // 2] = eg_v[0 : depth // 2, 0:nodes] + top
    gm_v[depth // 2 : depth] = eg_v[depth // 2 : depth, 0:nodes] + bottom
    gm_store = pltpu.make_async_copy(gm_v, gm_out.at[0], store_sem.at[0])
    gm_store.start()

    total = sum_v[yi]
    for copy in s2:
        copy.wait_recv()
    sent.extend(s2)
    for s in range(ny - 1):
        total = total + s2_r[s].astype(F32)
    s3_s[...] = total.astype(BF16)
    here = zh * nl + zl

    def s3_copy(z_, c_, slot):
        return pltpu.make_async_remote_copy(
            src_ref=s3_s, dst_ref=s3_r.at[slot],
            send_sem=s3_send.at[z_ * 2 + c_], recv_sem=s3_recv.at[slot],
            device_id=at(zh_=z_, core_=c_, zl_=core), device_id_type=MESH,
        )

    def is_me(z_, l_, c_):
        return (zh == z_) & (zl == l_) & (core == c_)

    for z_ in range(4):
        for c_ in range(2):

            @pl.when(jnp.logical_not(is_me(z_, core, c_)))
            def _():
                s3_copy(z_, c_, here).start()

            @pl.when(is_me(z_, core, c_))
            def _():
                s3_r[here] = s3_s[...]

    for z_ in range(4):
        for l_ in range(nl):

            @pl.when(jnp.logical_not(is_me(z_, l_, zl)))
            def _():
                s3_copy(0, 0, z_ * nl + l_).wait_recv()

    total = s3_r[0].astype(F32)
    for z_ in range(1, 4 * nl):
        total = total + s3_r[z_].astype(F32)
    gh_v[...] = jnp.concatenate([total[:per_y, 0:half], total[per_y:, 0 : depth - half]], axis=1)
    second = total[per_y:, depth - half : width - half]
    lane = lax.broadcasted_iota(jnp.int32, second.shape, 1)
    tail = jnp.where((lane >= MAIN) & (lane < MAIN + EXTRA), second, 0.0)
    folded = tail
    for b in range(1, BLOCKS):
        folded = folded + pltpu.roll(tail, LANES - 4 * b, 1)
    go_v[...] = jnp.where(lane < MAIN, second, folded)[:, : go_v.shape[1]]
    gh_store = pltpu.make_async_copy(gh_v, gh_out, store_sem.at[1])
    go_store = pltpu.make_async_copy(go_v, go_out, store_sem.at[2])
    gh_store.start()
    go_store.start()

    halo_down.wait_send()
    halo_up.wait_send()
    for copy in sent:
        copy.wait_send()
    for chunk in range(CHUNKS):
        keeper = keepers[chunk]

        @pl.when(member != keeper)
        def _():
            pext_copy(chunk).wait_send()

        @pl.when(member == keeper)
        def _():
            for j in range(8):
                if j != keeper:
                    gext_copy(chunk, j).wait_send()

    for z_ in range(4):
        for c_ in range(2):

            @pl.when(jnp.logical_not(is_me(z_, core, c_)))
            def _():
                s3_copy(z_, c_, here).wait_send()

    gm_store.wait()
    gh_store.wait()
    go_store.wait()


def solution(mesh, dims=(4, 2, 8)):
    def local(mesh_latent, grid_latent, edge_sources, edge_weights, area_weight, band_counts, target, hidden_weight, out_weight):
        nx, nl, ny = dims
        _, depth, nodes = mesh_latent.shape
        points = grid_latent.shape[2]
        per_chunk = points // CHUNKS
        variables = target.shape[0]
        per_x, per_z, per_y = depth // nx, depth // (nx * nl), depth // (nx * nl * ny)
        width = depth + LANES
        area = area_weight.reshape(1, points)
        vm, dma = pltpu.VMEM, pltpu.SemaphoreType.DMA
        scratch = [
            vm((depth, nodes), BF16), vm((depth, points), BF16), vm((3, points), jnp.int32), vm((3, points), BF16),
            vm((1, points), F32), pltpu.SMEM((1,), jnp.int32), vm((variables, points), BF16), vm((depth, depth), BF16), vm((variables, depth), BF16),
            vm((104, points), F32), vm((1, points), F32), vm((depth, depth), BF16), vm((LANES, depth), F32), vm((depth, LANES), BF16), vm((LANES, depth), BF16),
            vm((depth, nodes + 2 * HALO), BF16), vm((nodes + 2 * HALO, points), BF16), vm((depth, points), BF16), vm((depth, points), BF16), vm((depth, points), F32),
            vm((2, depth // 2, LANES), BF16), vm((2, depth // 2, LANES), BF16), vm((2, depth // 2, LANES), BF16), vm((2, depth // 2, LANES), BF16),
            vm((CHUNKS, BLOCKS, MAIN, LANES), BF16), vm((CHUNKS, EXTRA, LANES), BF16), vm((CHUNKS, 8, ROWS, LANES), BF16), vm((CHUNKS, 8, EXTRA, LANES), BF16),
            vm((CHUNKS, 8, ROWS, LANES), BF16), vm((CHUNKS, 8, EXTRA, LANES), BF16), vm((CHUNKS, BLOCKS, MAIN, LANES), BF16), vm((CHUNKS, EXTRA, LANES), BF16),
            vm((depth, width), F32), vm((depth, nodes + 2 * HALO), F32),
            vm((nx, per_z, width), BF16), vm((nx, per_z, width), BF16), vm((nx, per_z, width), BF16), vm((nx - 1, per_z, width), BF16),
            vm((ny, 2 * per_y, 3 * LANES), F32), vm((ny, 2 * per_y, 3 * LANES), BF16), vm((ny - 1, 2 * per_y, 3 * LANES), BF16),
            vm((2 * per_y, 3 * LANES), BF16), vm((4 * nl, 2 * per_y, 3 * LANES), BF16),
            vm((per_y, depth), F32), vm((per_y, variables), F32), vm((depth, nodes), F32),
            dma((9,)), dma((3,)), dma((2, 2)), dma((2, 2)), dma((2, 7 * CHUNKS)), dma((CHUNKS,)), dma((CHUNKS, 8)),
            dma((2, 7 * CHUNKS)), dma((CHUNKS, 8)), dma((CHUNKS,)),
            dma((2, 1)), dma((2, nx - 1)), dma((2, ny - 1)), dma((8,)), dma((4 * nl,)),
        ]
        return pl.pallas_call(
            functools.partial(kernel, dims),
            out_shape=(
                jax.ShapeDtypeStruct((per_y, depth), F32),
                jax.ShapeDtypeStruct((per_y, variables), F32),
                jax.ShapeDtypeStruct((1, depth, nodes), F32),
            ),
            in_specs=[pl.BlockSpec(memory_space=pl.ANY)] * 9,
            out_specs=[pl.BlockSpec(memory_space=pl.ANY)] * 3,
            scratch_shapes=scratch,
            compiler_params=pltpu.CompilerParams(
                collective_id=0, has_side_effects=True, vmem_limit_bytes=62 * 1024 * 1024
            ),
            name="step",
        )(mesh_latent, grid_latent, edge_sources, edge_weights, area, band_counts, target, hidden_weight, out_weight.T)

    return jax.shard_map(
        local,
        mesh=mesh,
        in_specs=(
            P("member", None, "grid"),
            P("member", None, "grid"),
            P(None, "grid"),
            P(None, "grid"),
            P("grid"),
            P("grid"),
            P(None, "grid"),
            P(),
            P(),
        ),
        out_specs=(P("grid", None), P("grid", None), P("member", None, "grid")),
        check_vma=False,
    )
```

```python
import functools

import jax
import jax.numpy as jnp
from jax import lax
from jax.experimental import pallas as pl
from jax.experimental.pallas import tpu as pltpu
from jax.sharding import PartitionSpec as P

HALO = 64
LANES = 128
CHUNKS = 4
BLOCKS = 2
GROUPS = 4
KEEPERS = (0, 4)
ROWS = 48
MAIN = 96
EXTRA = 16
MESH = pl.DeviceIdType.MESH

smooth_sq = 0.01
loss_scale = 4096.0

F32 = jnp.float32
BF16 = jnp.bfloat16


def slope(diff):
    return diff * lax.rsqrt(diff * diff + smooth_sq)


def dot(a, b, da, db):
    return lax.dot_general(a, b, (((da,), (db,)), ((), ())), preferred_element_type=F32)


def low_lanes(shape):
    return lax.broadcasted_iota(jnp.int32, shape, 1) < HALO


def pack(tile):
    half = tile.shape[0] // 2
    top, bottom = tile[:half], tile[half:]
    low = low_lanes(top.shape)
    down = jnp.where(low, top, pltpu.roll(bottom, HALO, 1))
    up = jnp.where(low, pltpu.roll(top, HALO, 1), bottom)
    return down, up


def unpack(below, above):
    low = low_lanes(below.shape)
    top = jnp.where(low, below, pltpu.roll(above, HALO, 1))
    bottom = jnp.where(low, pltpu.roll(below, HALO, 1), above)
    return top, bottom


def kernel(
    dims,
    mesh_in, grid_in, src_in, wgt_in, area_in, count_in, target_in, hw_in, ow_in,
    gh_out, go_out, gm_out,
    mesh_v, grid_v, src_v, wgt_v, area_v, count_v, tgt_v, hw_v, ow_v,
    tgt_f, coef_v, hw_t, ow_f, ow_r, ow_t, ext_v, adj_v, x_v, h_v, f_v,
    halo_s, halo_r, ghalo_s, ghalo_r,
    pred_s, pext_s, pred_r, pext_r, grad_s, gext_s, grad_r, gext_r,
    gw_v, eg_v, a0_s, a0_r, b0_s, b0_r, a1_f, a1_s, a1_r, b1_f, b1_s, b1_r, a2_f, a2_s, a2_r, b2_f, b2_s, b2_r, s3_s, s3_r,
    load_sem, halo_sem, ghalo_sem, p_send, p_recv, pe_send, pe_recv, g_send, g_recv, ge_send, ge_recv,
    s0_sem, a1_sem, b1_sem, a2_sem, b2_sem, s3_send, s3_recv,
):
    nx, nl, ny = dims
    nodes = mesh_v.shape[1]
    depth = hw_v.shape[0]
    width = depth + LANES
    points = grid_v.shape[1] // CHUNKS
    member, band = lax.axis_index("member"), lax.axis_index("grid")
    zh, core = member // 2, member % 2
    xi, zl, yi = band // (nl * ny), (band // ny) % nl, band % ny
    bands = nx * nl * ny

    def at(zh_=None, core_=None, x_=None, zl_=None, y_=None):
        zh_ = zh if zh_ is None else zh_
        core_ = core if core_ is None else core_
        x_ = xi if x_ is None else x_
        zl_ = zl if zl_ is None else zl_
        y_ = yi if y_ is None else y_
        return (zh_ * 2 + core_, x_ * (nl * ny) + zl_ * ny + y_)

    above = (member, (band + 1) % bands)
    below = (member, (band + bands - 1) % bands)

    def remote(src, dst, sems, i, device):
        return pltpu.make_async_remote_copy(
            src_ref=src, dst_ref=dst, send_sem=sems.at[0, i], recv_sem=sems.at[1, i],
            device_id=device, device_id_type=MESH,
        )

    barrier = pltpu.get_barrier_semaphore()
    partners = [
        at(zh_=(zh + a) % 4, core_=(core + b) % 2, zl_=(zl + c) % nl)
        for a in (2, 1, 3, 0) for b in range(2) for c in range(nl) if (a, b, c) != (0, 0, 0)
    ]
    partners += [at(y_=(yi + s) % ny) for s in range(1, ny)]
    partners += [at(x_=(xi + s) % nx) for s in range(1, nx)]
    partners += [above, below]

    def load(i, src, dst):
        copy = pltpu.make_async_copy(src, dst, load_sem.at[i])
        copy.start()
        return copy

    load_mesh = load(0, mesh_in.at[0], mesh_v)
    for partner in partners:
        pl.semaphore_signal(barrier, inc=1, device_id=partner, device_id_type=MESH)
    load_src = load(1, src_in, src_v)
    load_wgt = load(2, wgt_in, wgt_v)
    load_hw = load(3, hw_in, hw_v)
    load_ow = load(4, ow_in, ow_v)
    load_grid = load(5, grid_in.at[0], grid_v)
    load_area = load(6, area_in, area_v)
    load_tgt = load(7, target_in, tgt_v)
    load_count = load(8, count_in, count_v)

    load_mesh.wait()
    down, up = pack(mesh_v[...].astype(F32))
    halo_s[0] = down.astype(BF16)
    halo_s[1] = up.astype(BF16)
    pl.semaphore_wait(barrier, len(partners))
    halo_down = remote(halo_s.at[0], halo_r.at[0], halo_sem, 0, below)
    halo_up = remote(halo_s.at[1], halo_r.at[1], halo_sem, 1, above)
    halo_down.start()
    halo_up.start()

    ext_v[:, 0:nodes] = mesh_v[...]

    load_hw.wait()
    hw_t[...] = hw_v[...].astype(F32).T.astype(BF16)
    load_ow.wait()
    count = ow_v.shape[0]
    ow_f[MAIN:LANES] = jnp.zeros((LANES - MAIN, depth), F32)
    ow_f[0:count] = ow_v[...].astype(F32)
    tail = ow_f[MAIN : MAIN + 8]
    tail = tail + pltpu.roll(tail, 4, 0)
    ow_f[MAIN : MAIN + 8] = tail
    ow_f[MAIN + 8 : MAIN + 16] = tail
    ow_t[...] = ow_f[...].astype(BF16)
    ow_r[...] = ow_f[...].T.astype(BF16)

    load_src.wait()
    load_wgt.wait()
    row = lax.broadcasted_iota(jnp.int32, (nodes + 2 * HALO, points), 0)
    slot = jnp.where(row < nodes, row, jnp.where(row < nodes + HALO, row - (nodes + HALO), row - HALO))
    for chunk in range(CHUNKS):
        cols = pl.ds(chunk * points, points)
        adj = jnp.zeros(row.shape, F32)
        for k in range(3):
            source = src_v[pl.ds(k, 1), cols] - band * nodes
            weight = wgt_v[:, cols].astype(F32)[k : k + 1]
            adj = jnp.where(source == slot, weight, adj)
        adj_v[:, cols] = adj.astype(BF16)

    load_tgt.wait()
    tgt_f[0 : tgt_v.shape[0]] = tgt_v[...].astype(F32)
    load_area.wait()
    load_count.wait()
    place = lax.broadcasted_iota(jnp.int32, (1, CHUNKS * points), 1)
    live = (place < count_v[0]).astype(F32)
    coef_v[...] = loss_scale * area_v[...] * live / tgt_v.shape[0]
    group = lax.broadcasted_iota(jnp.int32, (EXTRA, LANES), 0) // 4

    def spread(blocks):
        out = blocks[0]
        for b in range(1, GROUPS):
            out = jnp.where(group == b, blocks[b], out)
        return out

    sent = []

    def finish(stage):
        if stage >= 2:
            halo_down.wait_send()
            halo_up.wait_send()
        for copy in sent:
            copy.wait_send()
        if stage >= 3:
            for k in range(CHUNKS):
                for a in range(1, 4):
                    pred_copy(k, (zh + a) % 4).wait_send()
                pl.when(core != k % 2)(functools.partial(left_pred, k))
                pl.when(core == k % 2)(functools.partial(left_grad, k))
            for sc in range(2):
                pl.when(member != KEEPERS[sc])(functools.partial(left_pext, sc))
                pl.when(member == KEEPERS[sc])(functools.partial(left_gext, sc))
        if stage >= 8:
            for z_ in range(4):
                for c_ in range(2):
                    pl.when(jnp.logical_not(is_me(z_, core, c_)))(functools.partial(left_s3, z_, c_))

    def left_pred(k):
        pred_copy(k, zh).wait_send()

    def left_grad(k):
        for i in range(1, 8):
            grad_copy(k, (member + i) % 8).wait_send()

    def left_pext(sc):
        pext_copy(sc).wait_send()

    def left_gext(sc):
        for j in range(8):
            if j != KEEPERS[sc]:
                gext_copy(sc, j).wait_send()

    def left_s3(z_, c_):
        s3_copy(z_, c_, here).wait_send()

    load_grid.wait()
    halo_down.wait_recv()
    halo_up.wait_recv()
    top, bottom = unpack(halo_r[1].astype(F32), halo_r[0].astype(F32))
    ext_v[0 : depth // 2, nodes : nodes + 2 * HALO] = top.astype(BF16)
    ext_v[depth // 2 : depth, nodes : nodes + 2 * HALO] = bottom.astype(BF16)

    def rows_of(z_):
        return pl.ds(pl.multiple_of(ROWS * (z_ // 2), 16), ROWS)

    def pred_copy(k, z_):
        return pltpu.make_async_remote_copy(
            src_ref=pred_s.at[k, z_ % 2, rows_of(z_)], dst_ref=pred_r.at[k // 2, member],
            send_sem=p_send.at[k, z_], recv_sem=p_recv.at[k // 2, member],
            device_id=at(zh_=z_, core_=k % 2), device_id_type=MESH,
        )

    def pred_arrival(k, j):
        return pltpu.make_async_remote_copy(
            src_ref=pred_s.at[k, 0, pl.ds(0, ROWS)], dst_ref=pred_r.at[k // 2, j],
            send_sem=p_send.at[k, 0], recv_sem=p_recv.at[k // 2, j],
            device_id=(j, band), device_id_type=MESH,
        )

    def grad_copy(k, j):
        return pltpu.make_async_remote_copy(
            src_ref=grad_s.at[k // 2, j], dst_ref=grad_r.at[k, zh % 2, rows_of(zh)],
            send_sem=g_send.at[k // 2, j], recv_sem=g_recv.at[k, zh],
            device_id=(j, band), device_id_type=MESH,
        )

    def grad_arrival(k, z_):
        return pltpu.make_async_remote_copy(
            src_ref=grad_s.at[0, 0], dst_ref=grad_r.at[k, z_ % 2, rows_of(z_)],
            send_sem=g_send.at[0, 0], recv_sem=g_recv.at[k, z_],
            device_id=at(zh_=z_, core_=k % 2), device_id_type=MESH,
        )

    def pext_copy(sc):
        return pltpu.make_async_remote_copy(
            src_ref=pext_s.at[sc], dst_ref=pext_r.at[member],
            send_sem=pe_send.at[sc], recv_sem=pe_recv.at[member],
            device_id=(KEEPERS[sc], band), device_id_type=MESH,
        )

    def pext_arrival(sc, j):
        return pltpu.make_async_remote_copy(
            src_ref=pext_s.at[sc], dst_ref=pext_r.at[j],
            send_sem=pe_send.at[sc], recv_sem=pe_recv.at[j],
            device_id=(j, band), device_id_type=MESH,
        )

    def gext_copy(sc, j):
        return pltpu.make_async_remote_copy(
            src_ref=gext_s.at[j], dst_ref=gext_r.at[sc],
            send_sem=ge_send.at[j], recv_sem=ge_recv.at[sc],
            device_id=(j, band), device_id_type=MESH,
        )

    tails = {}

    def forward(k):
        cols = pl.ds(k * points, points)
        agg = dot(ext_v[...], adj_v[:, cols], 1, 0)
        x_v[:, cols] = (agg + grid_v[:, cols].astype(F32)).astype(BF16)
        pre = dot(hw_t[...], x_v[:, cols], 1, 0)
        sig = 0.5 * jnp.tanh(0.5 * pre) + 0.5
        h_v[:, cols] = (pre * sig).astype(BF16)
        f_v[:, cols] = sig * (1.0 + pre * (1.0 - sig))
        pred = dot(ow_t[...], h_v[:, cols], 1, 0)
        for b in range(BLOCKS):
            block = pred[:, b * LANES : (b + 1) * LANES]
            pred_s[k, b] = block[:MAIN].astype(BF16)
            tails[k * BLOCKS + b] = block[MAIN : MAIN + EXTRA]
        for a in (2, 1, 3):
            pred_copy(k, (zh + a) % 4).start()

        @pl.when(core != k % 2)
        def _():
            pred_copy(k, zh).start()

        @pl.when(core == k % 2)
        def _():
            pred_r[k // 2, member] = pred_s[k, zh % 2, rows_of(zh)]

        if k % 2 == 1:
            sc = k // 2
            pext_s[sc] = spread([tails[sc * GROUPS + b] for b in range(GROUPS)]).astype(BF16)

            @pl.when(member != KEEPERS[sc])
            def _():
                pext_copy(sc).start()

    def fair(preds, target, weight):
        out = [slope(p - target) * (1.0 / 8.0) for p in preds]
        pairs = [jnp.zeros(target.shape, F32) for _ in preds]
        for i in range(8):
            for j in range(i + 1, 8):
                s = slope(preds[i] - preds[j])
                pairs[i] = pairs[i] + s
                pairs[j] = pairs[j] - s
        return [weight * (o - q * (1.0 / 56.0)) for o, q in zip(out, pairs)]

    def pair_up(k):
        @pl.when(core == k % 2)
        def _():
            for i in range(1, 8):
                pred_arrival(k, (member + i) % 8).wait_recv()
            lanes = pl.ds(pl.multiple_of(k * points + (zh % 2) * LANES, LANES), LANES)

            def tile(t, _):
                rows = pl.ds(pl.multiple_of(t * 16, 16), 16)
                target = tgt_f[pl.ds(pl.multiple_of(ROWS * (zh // 2) + t * 16, 16), 16), lanes]
                grads = fair([pred_r[k // 2, j, rows].astype(F32) for j in range(8)], target, coef_v[:, lanes])
                for j in range(8):
                    grad_s[k // 2, j, rows] = grads[j].astype(BF16)
                return 0

            lax.fori_loop(0, ROWS // 16, tile, 0)
            for i in (4, 5, 2, 3, 6, 7, 1):
                grad_copy(k, (member + i) % 8).start()
            grad_r[k, zh % 2, rows_of(zh)] = grad_s[k // 2, member]

    def pair_up_tail(sc):
        keeper = KEEPERS[sc]

        @pl.when(member == keeper)
        def _():
            pext_r[keeper] = pext_s[sc]
            for j in range(8):
                if j != keeper:
                    pext_arrival(sc, j).wait_recv()
            targets, weights = [], []
            row8 = lax.broadcasted_iota(jnp.int32, (8, LANES), 0)
            for b in range(GROUPS):
                at_b = pl.ds((sc * GROUPS + b) * LANES, LANES)
                tail = tgt_f[MAIN : MAIN + 8, at_b]
                tail = jnp.where(row8 < 4, tail, pltpu.roll(tail, 4, 0))
                targets.append(jnp.concatenate([tail, tail], axis=0))
                weights.append(jnp.broadcast_to(coef_v[:, at_b], (EXTRA, LANES)))
            grads = fair([pext_r[j].astype(F32) for j in range(8)], spread(targets), spread(weights))
            for j in range(8):
                gext_s[j] = grads[j].astype(BF16)
            for j in range(8):
                if j != keeper:
                    gext_copy(sc, j).start()
            gext_r[sc] = gext_s[keeper]

    def backward(k):
        cols = pl.ds(k * points, points)
        for a in range(1, 4):
            grad_arrival(k, (zh + a) % 4).wait_recv()

        @pl.when(core != k % 2)
        def _():
            grad_arrival(k, zh).wait_recv()

        sc = k // 2
        if k % 2 == 0:

            @pl.when(member != KEEPERS[sc])
            def _():
                gext_copy(sc, 0).wait_recv()

        tail = gext_r[sc].astype(F32)
        blocks = []
        for b in range(BLOCKS):
            mine = jnp.where(group == (k % 2) * BLOCKS + b, tail, 0.0).astype(BF16)
            blocks.append(jnp.concatenate([grad_r[k, b], mine, jnp.zeros((LANES - MAIN - EXTRA, LANES), BF16)], axis=0))
        gpred = jnp.concatenate(blocks, axis=1)
        dh = dot(ow_r[...], gpred, 1, 0)
        dpre = (dh * f_v[:, cols]).astype(BF16)
        return dpre, gpred

    def add(ref, where, value, first):
        if first:
            ref[:, where] = value
        else:
            ref[:, where] += value

    def weight_terms(k, dpre, gpred, left):
        cols = pl.ds(k * points, points)
        if left:
            add(gw_v, pl.ds(0, lead), dot(x_v[:, cols], dpre[:lead], 1, 1), k == 0)
        else:
            add(gw_v, pl.ds(lead, depth - lead), dot(x_v[:, cols], dpre[lead:], 1, 1), k == 0)
            add(gw_v, pl.ds(depth, LANES), dot(h_v[:, cols], gpred, 1, 1), k == 0)

    def node_sums(k, dpre):
        cols = pl.ds(k * points, points)
        dx = dot(hw_v[...], dpre, 1, 0).astype(BF16)
        add(eg_v, slice(None), dot(dx, adj_v[:, cols], 1, 1), k == 0)

    for k in range(CHUNKS):
        forward(k)
    for k in range(CHUNKS):
        pair_up(k)
        if k % 2 == 1:
            pair_up_tail(k // 2)
    lead = 2 * LANES
    per_x, per_z, per_y = depth // nx, depth // (nx * nl), depth // (nx * nl * ny)

    def part(x_, core_):
        return pl.ds(pl.multiple_of(x_ * per_x + core_ * per_z, 8), per_z)

    for k in range(CHUNKS - 1):
        dpre, gpred = backward(k)
        weight_terms(k, dpre, gpred, True)
        weight_terms(k, dpre, gpred, False)
        node_sums(k, dpre)
    last, gpred = backward(CHUNKS - 1)
    weight_terms(CHUNKS - 1, last, gpred, True)
    for x_ in range(nx):
        b0_s[x_] = gw_v[part(x_, 1 - core), 0:lead].astype(BF16)
    b0 = remote(b0_s, b0_r, s0_sem, 0, at(core_=1 - core))
    b0.start()
    weight_terms(CHUNKS - 1, last, gpred, False)
    for x_ in range(nx):
        a0_s[x_] = gw_v[part(x_, 1 - core), lead:width].astype(BF16)
    a0 = remote(a0_s, a0_r, s0_sem, 1, at(core_=1 - core))
    a0.start()
    sent.extend([b0, a0])

    b0.wait_recv()
    for x_ in range(nx):
        total = gw_v[part(x_, core), 0:lead] + b0_r[x_].astype(F32)
        for y_ in range(ny):
            b1_f[y_, x_ * per_y : (x_ + 1) * per_y] = total[y_ * per_y : (y_ + 1) * per_y]
    b1 = []
    for s in (4, 3, 5, 2, 6, 1, 7):
        if s < ny:
            y_ = (yi + s) % ny
            b1_s[y_] = b1_f[y_].astype(BF16)
            copy = remote(b1_s.at[y_], b1_r.at[s - 1], b1_sem, s - 1, at(y_=y_))
            copy.start()
            b1.append(copy)
    a0.wait_recv()
    for x_ in range(nx):
        a1_f[x_] = gw_v[part(x_, core), lead:width] + a0_r[x_].astype(F32)
    a1 = []
    for s in (2, 1, 3):
        if s < nx:
            x_ = (xi + s) % nx
            a1_s[x_] = a1_f[x_].astype(BF16)
            copy = remote(a1_s.at[x_], a1_r.at[s - 1], a1_sem, s - 1, at(x_=x_))
            copy.start()
            a1.append(copy)
    sent.extend(a1 + b1)

    node_sums(CHUNKS - 1, last)
    down, up = pack(eg_v[:, nodes : nodes + 2 * HALO])
    ghalo_s[0] = down.astype(BF16)
    ghalo_s[1] = up.astype(BF16)
    ghalo_down = remote(ghalo_s.at[0], ghalo_r.at[0], ghalo_sem, 0, below)
    ghalo_up = remote(ghalo_s.at[1], ghalo_r.at[1], ghalo_sem, 1, above)
    ghalo_down.start()
    ghalo_up.start()
    sent.extend([ghalo_down, ghalo_up])

    for copy in a1:
        copy.wait_recv()
    total = a1_f[xi]
    for s in range(nx - 1):
        total = total + a1_r[s].astype(F32)
    for y_ in range(ny):
        rows = total[y_ * per_y : (y_ + 1) * per_y]
        rest = jnp.concatenate([rows[:, lead:], jnp.zeros((per_y, LANES), F32)], axis=1)
        a2_f[y_] = jnp.concatenate([rows[:, :lead], rest], axis=0)
        a2_s[y_] = a2_f[y_].astype(BF16)
    a2 = []
    for s in (4, 3, 5, 2, 6, 1, 7):
        if s < ny:
            y_ = (yi + s) % ny
            copy = remote(a2_s.at[y_], a2_r.at[s - 1], a2_sem, s - 1, at(y_=y_))
            copy.start()
            a2.append(copy)
    for copy in b1:
        copy.wait_recv()
    total = b1_f[yi]
    for s in range(ny - 1):
        total = total + b1_r[s].astype(F32)
    for x_ in range(nx):
        rows = total[x_ * per_y : (x_ + 1) * per_y]
        b2_f[x_] = jnp.concatenate([rows[:, :LANES], rows[:, LANES:]], axis=0)
        b2_s[x_] = b2_f[x_].astype(BF16)
    b2 = []
    for s in (2, 1, 3):
        if s < nx:
            x_ = (xi + s) % nx
            copy = remote(b2_s.at[x_], b2_r.at[s - 1], b2_sem, s - 1, at(x_=x_))
            copy.start()
            b2.append(copy)
    sent.extend(a2 + b2)

    ghalo_down.wait_recv()
    ghalo_up.wait_recv()
    top, bottom = unpack(ghalo_r[1].astype(F32), ghalo_r[0].astype(F32))
    gm_out[0, 0 : depth // 2] = eg_v[0 : depth // 2, 0:nodes] + top
    gm_out[0, depth // 2 : depth] = eg_v[depth // 2 : depth, 0:nodes] + bottom

    for copy in b2:
        copy.wait_recv()
    total = b2_f[xi]
    for s in range(nx - 1):
        total = total + b2_r[s].astype(F32)
    s3_s[:, 0:LANES] = total.astype(BF16)
    for copy in a2:
        copy.wait_recv()
    total = a2_f[yi]
    for s in range(ny - 1):
        total = total + a2_r[s].astype(F32)
    s3_s[:, LANES : 3 * LANES] = total.astype(BF16)
    here = zh * nl + zl

    def s3_copy(z_, c_, slot):
        return pltpu.make_async_remote_copy(
            src_ref=s3_s, dst_ref=s3_r.at[slot],
            send_sem=s3_send.at[z_ * 2 + c_], recv_sem=s3_recv.at[slot],
            device_id=at(zh_=z_, core_=c_, zl_=core), device_id_type=MESH,
        )

    def is_me(z_, l_, c_):
        return (zh == z_) & (zl == l_) & (core == c_)

    for z_ in range(4):
        for c_ in range(2):

            @pl.when(jnp.logical_not(is_me(z_, core, c_)))
            def _():
                s3_copy(z_, c_, here).start()

            @pl.when(is_me(z_, core, c_))
            def _():
                s3_r[here] = s3_s[...]

    for z_ in range(4):
        for l_ in range(nl):

            @pl.when(jnp.logical_not(is_me(z_, l_, zl)))
            def _():
                s3_copy(0, 0, z_ * nl + l_).wait_recv()

    total = s3_r[0].astype(F32)
    for z_ in range(1, 4 * nl):
        total = total + s3_r[z_].astype(F32)
    gh_out[:, 0:LANES] = total[:per_y, 0:LANES]
    gh_out[:, LANES:lead] = total[per_y:, 0:LANES]
    gh_out[:, lead:depth] = total[:per_y, LANES : LANES + depth - lead]
    second = total[per_y:, LANES : 2 * LANES]
    lane = lax.broadcasted_iota(jnp.int32, second.shape, 1)
    tail = jnp.where((lane >= MAIN) & (lane < MAIN + EXTRA), second, 0.0)
    folded = tail
    for b in range(1, GROUPS):
        folded = folded + pltpu.roll(tail, LANES - 4 * b, 1)
    go_out[...] = jnp.where(lane < MAIN, second, folded)[:, : go_out.shape[1]]
    finish(99)


def flush(gh_in, go_in, gm_in, gh_out, go_out, gm_out, sem):
    copies = [pltpu.make_async_copy(a, b, sem.at[i]) for i, (a, b) in enumerate(((gm_in, gm_out), (gh_in, gh_out), (go_in, go_out)))]
    for copy in copies:
        copy.start()
    for copy in copies:
        copy.wait()


def solution(mesh, dims=(4, 2, 8)):
    def local(mesh_latent, grid_latent, edge_sources, edge_weights, area_weight, band_counts, target, hidden_weight, out_weight):
        nx, nl, ny = dims
        _, depth, nodes = mesh_latent.shape
        points = grid_latent.shape[2]
        variables = target.shape[0]
        per_x, per_z, per_y = depth // nx, depth // (nx * nl), depth // (nx * nl * ny)
        width, lead = depth + LANES, 2 * LANES
        tall = width - lead
        area = area_weight.reshape(1, points)
        vm, dma = pltpu.VMEM, pltpu.SemaphoreType.DMA
        scratch = [
            vm((depth, nodes), BF16), vm((depth, points), BF16), vm((3, points), jnp.int32), vm((3, points), BF16),
            vm((1, points), F32), pltpu.SMEM((1,), jnp.int32), vm((variables, points), BF16), vm((depth, depth), BF16), vm((variables, depth), BF16),
            vm((104, points), F32), vm((1, points), F32), vm((depth, depth), BF16), vm((LANES, depth), F32), vm((depth, LANES), BF16), vm((LANES, depth), BF16),
            vm((depth, nodes + 2 * HALO), BF16), vm((nodes + 2 * HALO, points), BF16), vm((depth, points), BF16), vm((depth, points), BF16), vm((depth, points), F32),
            vm((2, depth // 2, LANES), BF16), vm((2, depth // 2, LANES), BF16), vm((2, depth // 2, LANES), BF16), vm((2, depth // 2, LANES), BF16),
            vm((CHUNKS, BLOCKS, MAIN, LANES), BF16), vm((2, EXTRA, LANES), BF16), vm((2, 8, ROWS, LANES), BF16), vm((8, EXTRA, LANES), BF16),
            vm((2, 8, ROWS, LANES), BF16), vm((8, EXTRA, LANES), BF16), vm((CHUNKS, BLOCKS, MAIN, LANES), BF16), vm((2, EXTRA, LANES), BF16),
            vm((depth, width), F32), vm((depth, nodes + 2 * HALO), F32),
            vm((nx, per_z, tall), BF16), vm((nx, per_z, tall), BF16), vm((nx, per_z, lead), BF16), vm((nx, per_z, lead), BF16),
            vm((nx, per_z, tall), F32), vm((nx, per_z, tall), BF16), vm((nx - 1, per_z, tall), BF16),
            vm((ny, nx * per_y, lead), F32), vm((ny, nx * per_y, lead), BF16), vm((ny - 1, nx * per_y, lead), BF16),
            vm((ny, 2 * per_y, lead), F32), vm((ny, 2 * per_y, lead), BF16), vm((ny - 1, 2 * per_y, lead), BF16),
            vm((nx, 2 * per_y, LANES), F32), vm((nx, 2 * per_y, LANES), BF16), vm((nx - 1, 2 * per_y, LANES), BF16),
            vm((2 * per_y, 3 * LANES), BF16), vm((4 * nl, 2 * per_y, 3 * LANES), BF16),
            dma((9,)), dma((2, 2)), dma((2, 2)), dma((CHUNKS, 4)), dma((2, 8)), dma((2,)), dma((8,)),
            dma((2, 8)), dma((CHUNKS, 4)), dma((8,)), dma((2,)),
            dma((2, 2)), dma((2, nx - 1)), dma((2, ny - 1)), dma((2, ny - 1)), dma((2, nx - 1)), dma((8,)), dma((4 * nl,)),
        ]
        sums = pl.pallas_call(
            functools.partial(kernel, dims),
            out_shape=(
                pltpu.VMEM((per_y, depth), F32),
                pltpu.VMEM((per_y, variables), F32),
                pltpu.VMEM((1, depth, nodes), F32),
            ),
            in_specs=[pl.BlockSpec(memory_space=pl.ANY)] * 9,
            out_specs=[pl.BlockSpec(memory_space=pltpu.VMEM)] * 3,
            scratch_shapes=scratch,
            compiler_params=pltpu.CompilerParams(
                collective_id=0, has_side_effects=True, vmem_limit_bytes=62 * 1024 * 1024
            ),
            name="step",
        )(mesh_latent, grid_latent, edge_sources, edge_weights, area, band_counts, target, hidden_weight, out_weight.T)
        return pl.pallas_call(
            flush,
            out_shape=tuple(jax.ShapeDtypeStruct(a.shape, F32) for a in sums),
            in_specs=[pl.BlockSpec(memory_space=pl.ANY)] * 3,
            out_specs=[pl.BlockSpec(memory_space=pl.ANY)] * 3,
            scratch_shapes=[dma((3,))],
            compiler_params=pltpu.CompilerParams(vmem_limit_bytes=1024 * 1024),
            name="flush",
        )(*sums)

    return jax.shard_map(
        local,
        mesh=mesh,
        in_specs=(
            P("member", None, "grid"),
            P("member", None, "grid"),
            P(None, "grid"),
            P(None, "grid"),
            P("grid"),
            P("grid"),
            P(None, "grid"),
            P(),
            P(),
        ),
        out_specs=(P("grid", None), P("grid", None), P("member", None, "grid")),
        check_vma=False,
    )
```

```python
import functools

import jax
import jax.numpy as jnp
from jax import lax
from jax.experimental import pallas as pl
from jax.experimental.pallas import tpu as pltpu
from jax.sharding import PartitionSpec as P

HALO = 64
LANES = 128
CHUNKS = 4
BLOCKS = 2
GROUPS = 4
KEEPERS = (0, 4)
ROWS = 48
MAIN = 96
EXTRA = 16
MESH = pl.DeviceIdType.MESH

smooth_sq = 0.01
loss_scale = 4096.0

F32 = jnp.float32
BF16 = jnp.bfloat16


def slope(diff):
    return diff * lax.rsqrt(diff * diff + smooth_sq)


def dot(a, b, da, db):
    return lax.dot_general(a, b, (((da,), (db,)), ((), ())), preferred_element_type=F32)


def low_lanes(shape):
    return lax.broadcasted_iota(jnp.int32, shape, 1) < HALO


def pack(tile):
    half = tile.shape[0] // 2
    top, bottom = tile[:half], tile[half:]
    low = low_lanes(top.shape)
    down = jnp.where(low, top, pltpu.roll(bottom, HALO, 1))
    up = jnp.where(low, pltpu.roll(top, HALO, 1), bottom)
    return down, up


def unpack(below, above):
    low = low_lanes(below.shape)
    top = jnp.where(low, below, pltpu.roll(above, HALO, 1))
    bottom = jnp.where(low, pltpu.roll(below, HALO, 1), above)
    return top, bottom


def kernel(
    dims,
    mesh_in, grid_in, src_in, wgt_in, area_in, count_in, target_in, hw_in, ow_in,
    gh_out, go_out, gm_out,
    mesh_v, grid_v, src_v, wgt_v, area_v, count_v, tgt_v, hw_v, ow_v,
    tgt_f, coef_v, hw_t, ow_f, ow_r, ow_t, halo_v, hh_v, xo_v, po_v, adj_v, x_v, h_v, f_v,
    halo_s, halo_r, ghalo_s, ghalo_r,
    pred_s, pext_s, pred_r, pext_r, grad_s, gext_s, grad_r, gext_r,
    gw_v, eg_v, dpre_v, dx_v, gp_v, a0_s, a0_r, b0_s, b0_r, a1_f, a1_s, a1_r, b1_f, b1_s, b1_r, a2_f, a2_s, a2_r, b2_f, b2_s, b2_r, s3_s, s3_r,
    coef_r, ttail_s, ttail_r, tgt_r, t_sem, load_sem, halo_sem, ghalo_sem, p_send, p_recv, pe_send, pe_recv, g_send, g_recv, ge_send, ge_recv,
    s0_sem, a1_sem, b1_sem, a2_sem, b2_sem, s3_send, s3_recv,
):
    nx, nl, ny = dims
    nodes = mesh_v.shape[1]
    depth = hw_v.shape[0]
    width = depth + LANES
    points = grid_v.shape[1] // CHUNKS
    member, band = lax.axis_index("member"), lax.axis_index("grid")
    zh, core = member // 2, member % 2
    xi, zl, yi = band // (nl * ny), (band // ny) % nl, band % ny
    bands = nx * nl * ny

    def at(zh_=None, core_=None, x_=None, zl_=None, y_=None):
        zh_ = zh if zh_ is None else zh_
        core_ = core if core_ is None else core_
        x_ = xi if x_ is None else x_
        zl_ = zl if zl_ is None else zl_
        y_ = yi if y_ is None else y_
        return (zh_ * 2 + core_, x_ * (nl * ny) + zl_ * ny + y_)

    above = (member, (band + 1) % bands)
    below = (member, (band + bands - 1) % bands)

    def remote(src, dst, sems, i, device):
        return pltpu.make_async_remote_copy(
            src_ref=src, dst_ref=dst, send_sem=sems.at[0, i], recv_sem=sems.at[1, i],
            device_id=device, device_id_type=MESH,
        )

    barrier = pltpu.get_barrier_semaphore()
    other = xi * (nl * ny) + (1 - zl) * ny + yi
    ring = sorted(range(1, ny), key=lambda s: -min(s, ny - s))
    column = [(a, b, c) for a in (2, 1, 3, 0) for b in range(2) for c in range(nl) if (a, b, c) != (0, 0, 0)]
    partners = [at(zh_=(zh + a) % 4, core_=(core + b) % 2, zl_=(zl + c) % nl) for a, b, c in column[:4]]
    partners += [at(y_=(yi + s) % ny) for s in ring]
    partners += [above, below]
    partners += [at(zh_=(zh + a) % 4, core_=(core + b) % 2, zl_=(zl + c) % nl) for a, b, c in column[4:]]
    partners += [at(x_=(xi + s) % nx) for s in range(1, nx)]

    def load(i, src, dst):
        copy = pltpu.make_async_copy(src, dst, load_sem.at[i])
        copy.start()
        return copy

    load_mesh = load(0, mesh_in.at[0], mesh_v)
    for partner in partners:
        pl.semaphore_signal(barrier, inc=1, device_id=partner, device_id_type=MESH)
    load_src = load(1, src_in, src_v)
    load_wgt = load(2, wgt_in, wgt_v)
    load_hw = load(3, hw_in, hw_v)
    load_ow = load(4, ow_in, ow_v)
    load_grid = load(5, grid_in.at[0], grid_v)
    load_area = load(6, area_in, area_v)
    load_tgt = load(7, target_in, tgt_v)
    load_count = load(8, count_in, count_v)

    load_mesh.wait()
    down, up = pack(mesh_v[...].astype(F32))
    halo_s[0] = down.astype(BF16)
    halo_s[1] = up.astype(BF16)
    pl.semaphore_wait(barrier, len(partners))
    halo_down = remote(halo_s.at[0], halo_r.at[0], halo_sem, 0, below)
    halo_up = remote(halo_s.at[1], halo_r.at[1], halo_sem, 1, above)
    halo_down.start()
    halo_up.start()


    load_hw.wait()
    hw_t[...] = hw_v[...].astype(F32).T.astype(BF16)
    load_ow.wait()
    count = ow_v.shape[0]
    ow_f[MAIN:LANES] = jnp.zeros((LANES - MAIN, depth), F32)
    ow_f[0:count] = ow_v[...].astype(F32)
    tail = ow_f[MAIN : MAIN + 8]
    tail = tail + pltpu.roll(tail, 4, 0)
    ow_f[MAIN : MAIN + 8] = tail
    ow_f[MAIN + 8 : MAIN + 16] = tail
    ow_t[...] = ow_f[...].astype(BF16)
    ow_r[...] = ow_f[...].T.astype(BF16)

    load_src.wait()
    load_wgt.wait()
    row = lax.broadcasted_iota(jnp.int32, (nodes + 2 * HALO, points), 0)
    slot = jnp.where(row < nodes, row, jnp.where(row < nodes + HALO, row - (nodes + HALO), row - HALO))
    for chunk in range(CHUNKS):
        cols = pl.ds(chunk * points, points)
        adj = jnp.zeros(row.shape, F32)
        for k in range(3):
            source = src_v[pl.ds(k, 1), cols] - band * nodes
            weight = wgt_v[:, cols].astype(F32)[k : k + 1]
            adj = jnp.where(source == slot, weight, adj)
        adj_v[:, cols] = adj.astype(BF16)

    load_tgt.wait()
    tgt_f[0 : tgt_v.shape[0]] = tgt_v[...].astype(F32)
    load_area.wait()
    load_count.wait()
    place = lax.broadcasted_iota(jnp.int32, (1, CHUNKS * points), 1)
    live = (place < count_v[...]).astype(F32)
    coef_v[...] = loss_scale * area_v[...] * live / tgt_v.shape[0]
    group = lax.broadcasted_iota(jnp.int32, (EXTRA, LANES), 0) // 4

    def spread(blocks):
        out = blocks[0]
        for b in range(1, GROUPS):
            out = jnp.where(group == b, blocks[b], out)
        return out

    def rows_of(z_):
        return pl.ds(pl.multiple_of(ROWS * (z_ // 2), 16), ROWS)

    row8 = lax.broadcasted_iota(jnp.int32, (8, LANES), 0)
    for sc in range(2):
        targets = []
        for b in range(GROUPS):
            tail = tgt_f[MAIN : MAIN + 8, pl.ds((sc * GROUPS + b) * LANES, LANES)]
            tail = jnp.where(row8 < 4, tail, pltpu.roll(tail, 4, 0))
            targets.append(jnp.concatenate([tail, tail], axis=0))
        ttail_s[sc] = spread(targets).astype(BF16)
    mate = at(zl_=1 - zl)
    lent = [remote(coef_v, coef_r, t_sem, 0, mate), remote(ttail_s, ttail_r, t_sem, 1, mate)]
    for i in range(2):
        lanes = pl.ds(pl.multiple_of((2 * i + core) * points + (zh % 2) * LANES, LANES), LANES)
        lent.append(remote(tgt_v.at[rows_of(zh), lanes], tgt_r.at[i], t_sem, 2 + i, mate))
    for copy in lent:
        copy.start()

    turn = 1 + (ny - 2) * core
    sent = []

    def halos_left():
        halo_down.wait_send()
        halo_up.wait_send()

    def points_left():
        for k in range(CHUNKS):
            for z_ in range(4):
                pred_copy(k, z_).wait_send()
            pl.when(core == k % 2)(functools.partial(left_grad, k))
        for sc in range(2):
            pext_copy(sc).wait_send()
            pl.when(member == KEEPERS[sc])(functools.partial(left_gext, sc))

    def sent_left():
        for copy in sent:
            copy.wait_send()
        sent.clear()

    def last_left():
        for z_ in range(4):
            for c_ in range(2):
                pl.when(jnp.logical_not(is_me(z_, core, c_)))(functools.partial(left_s3, z_, c_))

    def left_grad(k):
        for j in range(8):
            grad_copy(k, j).wait_send()

    def left_gext(sc):
        for j in range(8):
            gext_copy(sc, j).wait_send()

    def left_s3(z_, c_):
        s3_copy(z_, c_, here).wait_send()

    load_grid.wait()
    for half in range(2):
        cols = pl.ds(half * 2 * points, 2 * points)
        xo_v[:, cols] = dot(mesh_v[...], adj_v[0:nodes, cols], 1, 0) + grid_v[:, cols].astype(F32)
        po_v[:, cols] = dot(hw_t[...], xo_v[:, cols].astype(BF16), 1, 0)
    halo_down.wait_recv()
    halo_up.wait_recv()
    top, bottom = unpack(halo_r[1].astype(F32), halo_r[0].astype(F32))
    halo_v[0 : depth // 2] = top.astype(BF16)
    halo_v[depth // 2 : depth] = bottom.astype(BF16)
    hh_v[...] = dot(hw_t[...], halo_v[...], 1, 0).astype(BF16)

    def toward(o):
        return (zh + zl + o + core * (3 - 2 * o)) % 4

    def pred_copy(k, z_):
        return pltpu.make_async_remote_copy(
            src_ref=pred_s.at[k, z_ % 2, rows_of(z_)], dst_ref=pred_r.at[k // 2, member],
            send_sem=p_send.at[k, z_], recv_sem=p_recv.at[k // 2, member],
            device_id=at(zh_=z_, core_=k % 2, zl_=1 - zl), device_id_type=MESH,
        )

    def pred_arrival(k, j):
        return pltpu.make_async_remote_copy(
            src_ref=pred_s.at[k, 0, pl.ds(0, ROWS)], dst_ref=pred_r.at[k // 2, j],
            send_sem=p_send.at[k, 0], recv_sem=p_recv.at[k // 2, j],
            device_id=(j, other), device_id_type=MESH,
        )

    def grad_copy(k, j):
        return pltpu.make_async_remote_copy(
            src_ref=grad_s.at[k // 2, j], dst_ref=grad_r.at[k, zh % 2, rows_of(zh)],
            send_sem=g_send.at[k // 2, j], recv_sem=g_recv.at[k, zh],
            device_id=(j, other), device_id_type=MESH,
        )

    def grad_arrival(k, z_):
        return pltpu.make_async_remote_copy(
            src_ref=grad_s.at[0, 0], dst_ref=grad_r.at[k, z_ % 2, rows_of(z_)],
            send_sem=g_send.at[0, 0], recv_sem=g_recv.at[k, z_],
            device_id=at(zh_=z_, core_=k % 2, zl_=1 - zl), device_id_type=MESH,
        )

    def pext_copy(sc):
        return pltpu.make_async_remote_copy(
            src_ref=pext_s.at[sc], dst_ref=pext_r.at[member],
            send_sem=pe_send.at[sc], recv_sem=pe_recv.at[member],
            device_id=(KEEPERS[sc], other), device_id_type=MESH,
        )

    def pext_arrival(sc, j):
        return pltpu.make_async_remote_copy(
            src_ref=pext_s.at[sc], dst_ref=pext_r.at[j],
            send_sem=pe_send.at[sc], recv_sem=pe_recv.at[j],
            device_id=(j, other), device_id_type=MESH,
        )

    def gext_copy(sc, j):
        return pltpu.make_async_remote_copy(
            src_ref=gext_s.at[j], dst_ref=gext_r.at[sc],
            send_sem=ge_send.at[j], recv_sem=ge_recv.at[sc],
            device_id=(j, other), device_id_type=MESH,
        )

    def forward(sc):
        cols = pl.ds(sc * 2 * points, 2 * points)
        pre = po_v[:, cols] + dot(hh_v[...], adj_v[nodes : nodes + 2 * HALO, cols], 1, 0)
        sig = 0.5 * jnp.tanh(0.5 * pre) + 0.5
        h_v[:, cols] = (pre * sig).astype(BF16)
        f_v[:, cols] = sig * (1.0 + pre * (1.0 - sig))
        pred = dot(ow_t[...], h_v[:, cols], 1, 0)
        tails = []
        for b in range(GROUPS):
            block = pred[:, b * LANES : (b + 1) * LANES]
            pred_s[2 * sc + b // BLOCKS, b % BLOCKS] = block[:MAIN].astype(BF16)
            tails.append(block[MAIN : MAIN + EXTRA])
        pext_s[sc] = spread(tails).astype(BF16)
        for k in (2 * sc, 2 * sc + 1):
            for o in (1, 2, 0, 3):
                pred_copy(k, toward(o)).start()
        pext_copy(sc).start()

    def fair(preds, target, weight):
        out = [slope(p - target) * (1.0 / 8.0) for p in preds]
        pairs = [jnp.zeros(target.shape, F32) for _ in preds]
        for i in range(8):
            for j in range(i + 1, 8):
                s = slope(preds[i] - preds[j])
                pairs[i] = pairs[i] + s
                pairs[j] = pairs[j] - s
        return [weight * (o - q * (1.0 / 56.0)) for o, q in zip(out, pairs)]

    def pair_up(k):
        @pl.when(core == k % 2)
        def _():
            for j in range(8):
                pred_arrival(k, j).wait_recv()
            weight = coef_r[:, pl.ds(pl.multiple_of(k * points + (zh % 2) * LANES, LANES), LANES)]

            def tile(t, _):
                rows = pl.ds(pl.multiple_of(t * 16, 16), 16)
                target = tgt_r[k // 2, rows].astype(F32)
                grads = fair([pred_r[k // 2, j, rows].astype(F32) for j in range(8)], target, weight)
                for j in range(8):
                    grad_s[k // 2, j, rows] = grads[j].astype(BF16)
                return 0

            lax.fori_loop(0, ROWS // 16, tile, 0)
            for o in (1, 2, 0, 3):
                for c_ in range(2):
                    grad_copy(k, toward(o) * 2 + c_).start()

    def pair_up_tail(sc):
        keeper = KEEPERS[sc]

        @pl.when(member == keeper)
        def _():
            for j in range(8):
                pext_arrival(sc, j).wait_recv()
            weights = []
            for b in range(GROUPS):
                at_b = pl.ds((sc * GROUPS + b) * LANES, LANES)
                weights.append(jnp.broadcast_to(coef_r[:, at_b], (EXTRA, LANES)))
            grads = fair([pext_r[j].astype(F32) for j in range(8)], ttail_r[sc].astype(F32), spread(weights))
            for j in range(8):
                gext_s[j] = grads[j].astype(BF16)
            for j in range(8):
                gext_copy(sc, j).start()

    def backward(sc):
        cols = pl.ds(sc * 2 * points, 2 * points)
        for k in (2 * sc, 2 * sc + 1):
            for z_ in range(4):
                grad_arrival(k, z_).wait_recv()
        gext_copy(sc, 0).wait_recv()

        tail = gext_r[sc].astype(F32)
        blocks = []
        for b in range(GROUPS):
            mine = jnp.where(group == b, tail, 0.0).astype(BF16)
            main = grad_r[2 * sc + b // BLOCKS, b % BLOCKS]
            blocks.append(jnp.concatenate([main, mine, jnp.zeros((LANES - MAIN - EXTRA, LANES), BF16)], axis=0))
        gpred = jnp.concatenate(blocks, axis=1)
        dh = dot(ow_r[...], gpred, 1, 0)
        dpre_v[:, cols] = (dh * f_v[:, cols]).astype(BF16)
        gp_v[:, cols] = gpred

    forward(0)
    forward(1)
    for half in range(2):
        cols = pl.ds(half * 2 * points, 2 * points)
        x_v[:, cols] = (xo_v[:, cols] + dot(halo_v[...], adj_v[nodes : nodes + 2 * HALO, cols], 1, 0)).astype(BF16)
    for copy in lent:
        copy.wait_recv()
    sent.extend(lent)
    for k in range(CHUNKS):
        pair_up(k)
        if k % 2 == 1:
            pair_up_tail(k // 2)
    lead = 2 * LANES
    per_x, per_z, per_y = depth // nx, depth // (nx * nl), depth // (nx * nl * ny)

    def part(x_, core_):
        return pl.ds(pl.multiple_of(x_ * per_x + core_ * per_z, 8), per_z)

    backward(0)
    early, late = pl.ds(0, 2 * points), pl.ds(2 * points, 2 * points)
    gw_v[:, 0:depth] = dot(x_v[:, early], dpre_v[:, early], 1, 1)
    gw_v[:, depth:width] = dot(h_v[:, early], gp_v[:, early], 1, 1)
    backward(1)
    gw_v[:, 0:lead] += dot(x_v[:, late], dpre_v[0:lead, late], 1, 1)
    for x_ in range(nx):
        b0_s[x_] = gw_v[part(x_, 1 - core), 0:lead].astype(BF16)
    b0 = remote(b0_s, b0_r, s0_sem, 0, at(core_=1 - core))
    b0.start()
    gw_v[:, lead:depth] += dot(x_v[:, late], dpre_v[lead:depth, late], 1, 1)
    gw_v[:, depth:width] += dot(h_v[:, late], gp_v[:, late], 1, 1)
    for x_ in range(nx):
        a0_s[x_] = gw_v[part(x_, 1 - core), lead:width].astype(BF16)
    a0 = remote(a0_s, a0_r, s0_sem, 1, at(core_=1 - core))
    a0.start()
    sent.extend([b0, a0])

    b0.wait_recv()
    for x_ in range(nx):
        total = gw_v[part(x_, core), 0:lead] + b0_r[x_].astype(F32)
        for y_ in range(ny):
            b1_f[y_, x_ * per_y : (x_ + 1) * per_y] = total[y_ * per_y : (y_ + 1) * per_y]
    b1 = []
    for s in (4, 3, 5, 2, 6, 1, 7):
        if s < ny:
            y_ = (yi + s * turn) % ny
            b1_s[y_] = b1_f[y_].astype(BF16)
            copy = remote(b1_s.at[y_], b1_r.at[s - 1], b1_sem, s - 1, at(y_=y_))
            copy.start()
            b1.append(copy)
    a0.wait_recv()
    for x_ in range(nx):
        a1_f[x_] = gw_v[part(x_, core), lead:width] + a0_r[x_].astype(F32)
    a1 = []
    for s in (2, 1, 3):
        if s < nx:
            x_ = (xi + s * (1 + (nx - 2) * core)) % nx
            a1_s[x_] = a1_f[x_].astype(BF16)
            copy = remote(a1_s.at[x_], a1_r.at[s - 1], a1_sem, s - 1, at(x_=x_))
            copy.start()
            a1.append(copy)
    sent.extend(a1 + b1)

    for half in range(2):
        cols = pl.ds(half * 2 * points, 2 * points)
        dx_v[:, cols] = dot(hw_v[...], dpre_v[:, cols], 1, 0).astype(BF16)
    down, up = pack(dot(dx_v[...], adj_v[nodes : nodes + 2 * HALO], 1, 1))
    ghalo_s[0] = down.astype(BF16)
    ghalo_s[1] = up.astype(BF16)
    ghalo_down = remote(ghalo_s.at[0], ghalo_r.at[0], ghalo_sem, 0, below)
    ghalo_up = remote(ghalo_s.at[1], ghalo_r.at[1], ghalo_sem, 1, above)
    ghalo_down.start()
    ghalo_up.start()
    sent.extend([ghalo_down, ghalo_up])
    eg_v[...] = dot(dx_v[...], adj_v[0:nodes], 1, 1)
    halos_left()
    points_left()

    for copy in a1:
        copy.wait_recv()
    total = a1_f[xi]
    for s in range(nx - 1):
        total = total + a1_r[s].astype(F32)
    for y_ in range(ny):
        rows = total[y_ * per_y : (y_ + 1) * per_y]
        rest = jnp.concatenate([rows[:, lead:], jnp.zeros((per_y, LANES), F32)], axis=1)
        a2_f[y_] = jnp.concatenate([rows[:, :lead], rest], axis=0)
        a2_s[y_] = a2_f[y_].astype(BF16)
    a2 = []
    for s in (4, 3, 5, 2, 6, 1, 7):
        if s < ny:
            y_ = (yi + s * turn) % ny
            copy = remote(a2_s.at[y_], a2_r.at[s - 1], a2_sem, s - 1, at(y_=y_))
            copy.start()
            a2.append(copy)
    for copy in b1:
        copy.wait_recv()
    total = b1_f[yi]
    for s in range(ny - 1):
        total = total + b1_r[s].astype(F32)
    for x_ in range(nx):
        rows = total[x_ * per_y : (x_ + 1) * per_y]
        b2_f[x_] = jnp.concatenate([rows[:, :LANES], rows[:, LANES:]], axis=0)
        b2_s[x_] = b2_f[x_].astype(BF16)
    b2 = []
    for s in (2, 1, 3):
        if s < nx:
            x_ = (xi + s * (1 + (nx - 2) * core)) % nx
            copy = remote(b2_s.at[x_], b2_r.at[s - 1], b2_sem, s - 1, at(x_=x_))
            copy.start()
            b2.append(copy)
    sent_left()
    sent.extend(a2 + b2)

    ghalo_down.wait_recv()
    ghalo_up.wait_recv()
    top, bottom = unpack(ghalo_r[1].astype(F32), ghalo_r[0].astype(F32))
    gm_out[0, 0 : depth // 2] = eg_v[0 : depth // 2] + top
    gm_out[0, depth // 2 : depth] = eg_v[depth // 2 : depth] + bottom

    for copy in b2:
        copy.wait_recv()
    total = b2_f[xi]
    for s in range(nx - 1):
        total = total + b2_r[s].astype(F32)
    s3_s[:, 0:LANES] = total.astype(BF16)
    for copy in a2:
        copy.wait_recv()
    total = a2_f[yi]
    for s in range(ny - 1):
        total = total + a2_r[s].astype(F32)
    s3_s[:, LANES : 3 * LANES] = total.astype(BF16)
    here = zh * nl + zl

    def s3_copy(z_, c_, slot):
        return pltpu.make_async_remote_copy(
            src_ref=s3_s, dst_ref=s3_r.at[slot],
            send_sem=s3_send.at[z_ * 2 + c_], recv_sem=s3_recv.at[slot],
            device_id=at(zh_=z_, core_=c_, zl_=core), device_id_type=MESH,
        )

    def is_me(z_, l_, c_):
        return (zh == z_) & (zl == l_) & (core == c_)

    for z_ in range(4):
        for c_ in range(2):

            @pl.when(jnp.logical_not(is_me(z_, core, c_)))
            def _():
                s3_copy(z_, c_, here).start()

            @pl.when(is_me(z_, core, c_))
            def _():
                s3_r[here] = s3_s[...]

    sent_left()
    for z_ in range(4):
        for l_ in range(nl):

            @pl.when(jnp.logical_not(is_me(z_, l_, zl)))
            def _():
                s3_copy(0, 0, z_ * nl + l_).wait_recv()

    total = s3_r[0].astype(F32)
    for z_ in range(1, 4 * nl):
        total = total + s3_r[z_].astype(F32)
    gh_out[:, 0:LANES] = total[:per_y, 0:LANES]
    gh_out[:, LANES:lead] = total[per_y:, 0:LANES]
    gh_out[:, lead:depth] = total[:per_y, LANES : LANES + depth - lead]
    second = total[per_y:, LANES : 2 * LANES]
    lane = lax.broadcasted_iota(jnp.int32, second.shape, 1)
    tail = jnp.where((lane >= MAIN) & (lane < MAIN + EXTRA), second, 0.0)
    folded = tail
    for b in range(1, GROUPS):
        folded = folded + pltpu.roll(tail, LANES - 4 * b, 1)
    go_out[...] = jnp.where(lane < MAIN, second, folded)[:, : go_out.shape[1]]
    last_left()


def flush(gh_in, go_in, gm_in, gh_out, go_out, gm_out, sem):
    copies = [pltpu.make_async_copy(a, b, sem.at[i]) for i, (a, b) in enumerate(((gm_in, gm_out), (gh_in, gh_out), (go_in, go_out)))]
    for copy in copies:
        copy.start()
    for copy in copies:
        copy.wait()


def solution(mesh, dims=(4, 2, 8)):
    def local(mesh_latent, grid_latent, edge_sources, edge_weights, area_weight, band_counts, target, hidden_weight, out_weight):
        nx, nl, ny = dims
        _, depth, nodes = mesh_latent.shape
        points = grid_latent.shape[2]
        variables = target.shape[0]
        per_x, per_z, per_y = depth // nx, depth // (nx * nl), depth // (nx * nl * ny)
        width, lead = depth + LANES, 2 * LANES
        tall = width - lead
        area = area_weight.reshape(1, points)
        vm, dma = pltpu.VMEM, pltpu.SemaphoreType.DMA
        scratch = [
            vm((depth, nodes), BF16), vm((depth, points), BF16), vm((3, points), jnp.int32), vm((3, points), BF16),
            vm((1, points), F32), vm((1, 1), jnp.int32), vm((variables, points), BF16), vm((depth, depth), BF16), vm((variables, depth), BF16),
            vm((104, points), F32), vm((1, points), F32), vm((depth, depth), BF16), vm((LANES, depth), F32), vm((depth, LANES), BF16), vm((LANES, depth), BF16),
            vm((depth, 2 * HALO), BF16), vm((depth, 2 * HALO), BF16), vm((depth, points), F32), vm((depth, points), F32),
            vm((nodes + 2 * HALO, points), BF16), vm((depth, points), BF16), vm((depth, points), BF16), vm((depth, points), F32),
            vm((2, depth // 2, LANES), BF16), vm((2, depth // 2, LANES), BF16), vm((2, depth // 2, LANES), BF16), vm((2, depth // 2, LANES), BF16),
            vm((CHUNKS, BLOCKS, MAIN, LANES), BF16), vm((2, EXTRA, LANES), BF16), vm((2, 8, ROWS, LANES), BF16), vm((8, EXTRA, LANES), BF16),
            vm((2, 8, ROWS, LANES), BF16), vm((8, EXTRA, LANES), BF16), vm((CHUNKS, BLOCKS, MAIN, LANES), BF16), vm((2, EXTRA, LANES), BF16),
            vm((depth, width), F32), vm((depth, nodes), F32), vm((depth, points), BF16), vm((depth, points), BF16), vm((LANES, points), BF16),
            vm((nx, per_z, tall), BF16), vm((nx, per_z, tall), BF16), vm((nx, per_z, lead), BF16), vm((nx, per_z, lead), BF16),
            vm((nx, per_z, tall), F32), vm((nx, per_z, tall), BF16), vm((nx - 1, per_z, tall), BF16),
            vm((ny, nx * per_y, lead), F32), vm((ny, nx * per_y, lead), BF16), vm((ny - 1, nx * per_y, lead), BF16),
            vm((ny, 2 * per_y, lead), F32), vm((ny, 2 * per_y, lead), BF16), vm((ny - 1, 2 * per_y, lead), BF16),
            vm((nx, 2 * per_y, LANES), F32), vm((nx, 2 * per_y, LANES), BF16), vm((nx - 1, 2 * per_y, LANES), BF16),
            vm((2 * per_y, 3 * LANES), BF16), vm((4 * nl, 2 * per_y, 3 * LANES), BF16),
            vm((1, points), F32), vm((2, EXTRA, LANES), BF16), vm((2, EXTRA, LANES), BF16), vm((2, ROWS, LANES), BF16), dma((2, 4)),
            dma((9,)), dma((2, 2)), dma((2, 2)), dma((CHUNKS, 4)), dma((2, 8)), dma((2,)), dma((8,)),
            dma((2, 8)), dma((CHUNKS, 4)), dma((8,)), dma((2,)),
            dma((2, 2)), dma((2, nx - 1)), dma((2, ny - 1)), dma((2, ny - 1)), dma((2, nx - 1)), dma((8,)), dma((4 * nl,)),
        ]
        sums = pl.pallas_call(
            functools.partial(kernel, dims),
            out_shape=(
                pltpu.VMEM((per_y, depth), F32),
                pltpu.VMEM((per_y, variables), F32),
                pltpu.VMEM((1, depth, nodes), F32),
            ),
            in_specs=[pl.BlockSpec(memory_space=pl.ANY)] * 9,
            out_specs=[pl.BlockSpec(memory_space=pltpu.VMEM)] * 3,
            scratch_shapes=scratch,
            compiler_params=pltpu.CompilerParams(
                collective_id=0, has_side_effects=True, vmem_limit_bytes=62 * 1024 * 1024
            ),
            name="step",
        )(mesh_latent, grid_latent, edge_sources, edge_weights, area, band_counts.reshape(1, 1), target, hidden_weight, out_weight.T)
        return pl.pallas_call(
            flush,
            out_shape=tuple(jax.ShapeDtypeStruct(a.shape, F32) for a in sums),
            in_specs=[pl.BlockSpec(memory_space=pl.ANY)] * 3,
            out_specs=[pl.BlockSpec(memory_space=pl.ANY)] * 3,
            scratch_shapes=[dma((3,))],
            compiler_params=pltpu.CompilerParams(vmem_limit_bytes=1024 * 1024),
            name="flush",
        )(*sums)

    return jax.shard_map(
        local,
        mesh=mesh,
        in_specs=(
            P("member", None, "grid"),
            P("member", None, "grid"),
            P(None, "grid"),
            P(None, "grid"),
            P("grid"),
            P("grid"),
            P(None, "grid"),
            P(),
            P(),
        ),
        out_specs=(P("grid", None), P("grid", None), P("member", None, "grid")),
        check_vma=False,
    )
```

```python
import functools

import jax
import jax.numpy as jnp
from jax import lax
from jax.experimental import pallas as pl
from jax.experimental.pallas import tpu as pltpu
from jax.sharding import PartitionSpec as P

HALO = 64
LANES = 128
CHUNKS = 4
BLOCKS = 2
GROUPS = 4
KEEPERS = (0, 4)
ROWS = 48
MAIN = 96
EXTRA = 16
MESH = pl.DeviceIdType.MESH

smooth_sq = 0.01
loss_scale = 4096.0

F32 = jnp.float32
BF16 = jnp.bfloat16


def slope(diff):
    return diff * lax.rsqrt(diff * diff + smooth_sq)


def dot(a, b, da, db):
    return lax.dot_general(a, b, (((da,), (db,)), ((), ())), preferred_element_type=F32)


def low_lanes(shape):
    return lax.broadcasted_iota(jnp.int32, shape, 1) < HALO


def pack(tile):
    half = tile.shape[0] // 2
    top, bottom = tile[:half], tile[half:]
    low = low_lanes(top.shape)
    down = jnp.where(low, top, pltpu.roll(bottom, HALO, 1))
    up = jnp.where(low, pltpu.roll(top, HALO, 1), bottom)
    return down, up


def unpack(below, above):
    low = low_lanes(below.shape)
    top = jnp.where(low, below, pltpu.roll(above, HALO, 1))
    bottom = jnp.where(low, pltpu.roll(below, HALO, 1), above)
    return top, bottom


def kernel(
    dims,
    mesh_in, grid_in, src_in, wgt_in, area_in, count_in, target_in, hw_in, ow_in,
    gh_out, go_out, gm_out,
    mesh_v, grid_v, src_v, wgt_v, area_v, count_v, tgt_v, hw_v, ow_v,
    tgt_f, coef_v, hw_t, ow_f, ow_r, ow_t, halo_v, hh_v, xo_v, po_v, adj_v, x_v, h_v, f_v,
    halo_s, halo_r, ghalo_s, ghalo_r,
    pred_s, pext_s, pred_r, pext_r, grad_s, gext_s, grad_r, gext_r,
    gw_v, eg_v, dpre_v, dx_v, gp_v, a0_s, a0_r, b0_s, b0_r, a1_f, a1_s, a1_r, b1_f, b1_s, b1_r, a2_f, a2_s, a2_r, b2_f, b2_s, b2_r, s3_s, s3_r,
    near_sem, coef_r, ttail_s, ttail_r, tgt_r, t_sem, load_sem, halo_sem, ghalo_sem, p_send, p_recv, pe_send, pe_recv, g_send, g_recv, ge_send, ge_recv,
    s0_sem, a1_sem, b1_sem, a2_sem, b2_sem, s3_send, s3_recv,
):
    nx, nl, ny = dims
    nodes = mesh_v.shape[1]
    depth = hw_v.shape[0]
    width = depth + LANES
    points = grid_v.shape[1] // CHUNKS
    member, band = lax.axis_index("member"), lax.axis_index("grid")
    zh, core = member // 2, member % 2
    xi, zl, yi = band // (nl * ny), (band // ny) % nl, band % ny
    bands = nx * nl * ny

    def at(zh_=None, core_=None, x_=None, zl_=None, y_=None):
        zh_ = zh if zh_ is None else zh_
        core_ = core if core_ is None else core_
        x_ = xi if x_ is None else x_
        zl_ = zl if zl_ is None else zl_
        y_ = yi if y_ is None else y_
        return (zh_ * 2 + core_, x_ * (nl * ny) + zl_ * ny + y_)

    above = (member, (band + 1) % bands)
    below = (member, (band + bands - 1) % bands)

    def remote(src, dst, sems, i, device):
        return pltpu.make_async_remote_copy(
            src_ref=src, dst_ref=dst, send_sem=sems.at[0, i], recv_sem=sems.at[1, i],
            device_id=device, device_id_type=MESH,
        )

    barrier = pltpu.get_barrier_semaphore()
    other = xi * (nl * ny) + (1 - zl) * ny + yi
    column = [(a, b, c) for a in (2, 1, 3, 0) for b in range(2) for c in range(nl) if (a, b, c) != (0, 0, 0)]
    beside = [at(y_=(yi + 1) % ny), at(y_=(yi + ny - 1) % ny), at(x_=(xi + 1) % nx), at(x_=(xi + nx - 1) % nx)]
    partners = [at(zh_=(zh + a) % 4, core_=(core + b) % 2, zl_=(zl + c) % nl) for a, b, c in column[:4]]
    partners += [above, below] + beside
    partners += [at(zh_=(zh + a) % 4, core_=(core + b) % 2, zl_=(zl + c) % nl) for a, b, c in column[4:]]

    def tell(i):
        for partner in beside if i == 0 else beside[:2]:
            pl.semaphore_signal(near_sem.at[i], inc=1, device_id=partner, device_id_type=MESH)

    def hear(i):
        pl.semaphore_wait(near_sem.at[i], 4 if i == 0 else 2)

    def load(i, src, dst):
        copy = pltpu.make_async_copy(src, dst, load_sem.at[i])
        copy.start()
        return copy

    load_mesh = load(0, mesh_in.at[0], mesh_v)
    for partner in partners:
        pl.semaphore_signal(barrier, inc=1, device_id=partner, device_id_type=MESH)
    load_src = load(1, src_in, src_v)
    load_wgt = load(2, wgt_in, wgt_v)
    load_hw = load(3, hw_in, hw_v)
    load_ow = load(4, ow_in, ow_v)
    load_grid = load(5, grid_in.at[0], grid_v)
    load_area = load(6, area_in, area_v)
    load_tgt = load(7, target_in, tgt_v)
    load_count = load(8, count_in, count_v)

    load_mesh.wait()
    down, up = pack(mesh_v[...].astype(F32))
    halo_s[0] = down.astype(BF16)
    halo_s[1] = up.astype(BF16)
    pl.semaphore_wait(barrier, len(partners))
    halo_down = remote(halo_s.at[0], halo_r.at[0], halo_sem, 0, below)
    halo_up = remote(halo_s.at[1], halo_r.at[1], halo_sem, 1, above)
    halo_down.start()
    halo_up.start()
    tell(0)


    load_hw.wait()
    hw_t[...] = hw_v[...].astype(F32).T.astype(BF16)
    load_ow.wait()
    count = ow_v.shape[0]
    ow_f[MAIN:LANES] = jnp.zeros((LANES - MAIN, depth), F32)
    ow_f[0:count] = ow_v[...].astype(F32)
    tail = ow_f[MAIN : MAIN + 8]
    tail = tail + pltpu.roll(tail, 4, 0)
    ow_f[MAIN : MAIN + 8] = tail
    ow_f[MAIN + 8 : MAIN + 16] = tail
    ow_t[...] = ow_f[...].astype(BF16)
    ow_r[...] = ow_f[...].T.astype(BF16)

    load_src.wait()
    load_wgt.wait()
    row = lax.broadcasted_iota(jnp.int32, (nodes + 2 * HALO, points), 0)
    slot = jnp.where(row < nodes, row, jnp.where(row < nodes + HALO, row - (nodes + HALO), row - HALO))
    for chunk in range(CHUNKS):
        cols = pl.ds(chunk * points, points)
        adj = jnp.zeros(row.shape, F32)
        for k in range(3):
            source = src_v[pl.ds(k, 1), cols] - band * nodes
            weight = wgt_v[:, cols].astype(F32)[k : k + 1]
            adj = jnp.where(source == slot, weight, adj)
        adj_v[:, cols] = adj.astype(BF16)

    load_tgt.wait()
    tgt_f[0 : tgt_v.shape[0]] = tgt_v[...].astype(F32)
    load_area.wait()
    load_count.wait()
    place = lax.broadcasted_iota(jnp.int32, (1, CHUNKS * points), 1)
    live = (place < count_v[...]).astype(F32)
    coef_v[...] = loss_scale * area_v[...] * live / tgt_v.shape[0]
    group = lax.broadcasted_iota(jnp.int32, (EXTRA, LANES), 0) // 4

    def spread(blocks):
        out = blocks[0]
        for b in range(1, GROUPS):
            out = jnp.where(group == b, blocks[b], out)
        return out

    def rows_of(z_):
        return pl.ds(pl.multiple_of(ROWS * (z_ // 2), 16), ROWS)

    row8 = lax.broadcasted_iota(jnp.int32, (8, LANES), 0)
    for sc in range(2):
        targets = []
        for b in range(GROUPS):
            tail = tgt_f[MAIN : MAIN + 8, pl.ds((sc * GROUPS + b) * LANES, LANES)]
            tail = jnp.where(row8 < 4, tail, pltpu.roll(tail, 4, 0))
            targets.append(jnp.concatenate([tail, tail], axis=0))
        ttail_s[sc] = spread(targets).astype(BF16)
    mate = at(zl_=1 - zl)
    lent = [remote(coef_v, coef_r, t_sem, 0, mate), remote(ttail_s, ttail_r, t_sem, 1, mate)]
    for i in range(2):
        lanes = pl.ds(pl.multiple_of((2 * i + core) * points + (zh % 2) * LANES, LANES), LANES)
        lent.append(remote(tgt_v.at[rows_of(zh), lanes], tgt_r.at[i], t_sem, 2 + i, mate))
    for copy in lent:
        copy.start()

    turn = 1 + (ny - 2) * core
    sent = []

    def halos_left():
        halo_down.wait_send()
        halo_up.wait_send()

    def points_left():
        for k in range(CHUNKS):
            for z_ in range(4):
                pred_copy(k, z_).wait_send()
            pl.when(core == k % 2)(functools.partial(left_grad, k))
        for sc in range(2):
            pext_copy(sc).wait_send()
            pl.when(member == KEEPERS[sc])(functools.partial(left_gext, sc))

    def sent_left():
        for copy in sent:
            copy.wait_send()
        sent.clear()

    def last_left():
        for a in range(4):
            for c_ in range(2):
                left = s3_copy((zh + a) % 4, c_, here)
                if a == 0:
                    pl.when(jnp.logical_not((zl == core) & (core == c_)))(left.wait_send)
                else:
                    left.wait_send()

    def left_grad(k):
        for j in range(8):
            grad_copy(k, j).wait_send()

    def left_gext(sc):
        for j in range(8):
            gext_copy(sc, j).wait_send()

    load_grid.wait()
    for half in range(2):
        cols = pl.ds(half * 2 * points, 2 * points)
        xo_v[:, cols] = dot(mesh_v[...], adj_v[0:nodes, cols], 1, 0) + grid_v[:, cols].astype(F32)
        po_v[:, cols] = dot(hw_t[...], xo_v[:, cols].astype(BF16), 1, 0)
    halo_down.wait_recv()
    halo_up.wait_recv()
    top, bottom = unpack(halo_r[1].astype(F32), halo_r[0].astype(F32))
    halo_v[0 : depth // 2] = top.astype(BF16)
    halo_v[depth // 2 : depth] = bottom.astype(BF16)
    hh_v[...] = dot(hw_t[...], halo_v[...], 1, 0).astype(BF16)

    def toward(o):
        return (zh + zl + o + core * (3 - 2 * o)) % 4

    def pred_copy(k, z_):
        return pltpu.make_async_remote_copy(
            src_ref=pred_s.at[k, z_ % 2, rows_of(z_)], dst_ref=pred_r.at[k // 2, member],
            send_sem=p_send.at[k, z_], recv_sem=p_recv.at[k // 2, member],
            device_id=at(zh_=z_, core_=k % 2, zl_=1 - zl), device_id_type=MESH,
        )

    def pred_arrival(k, j):
        return pltpu.make_async_remote_copy(
            src_ref=pred_s.at[k, 0, pl.ds(0, ROWS)], dst_ref=pred_r.at[k // 2, j],
            send_sem=p_send.at[k, 0], recv_sem=p_recv.at[k // 2, j],
            device_id=(j, other), device_id_type=MESH,
        )

    def grad_copy(k, j):
        return pltpu.make_async_remote_copy(
            src_ref=grad_s.at[k // 2, j], dst_ref=grad_r.at[k, zh % 2, rows_of(zh)],
            send_sem=g_send.at[k // 2, j], recv_sem=g_recv.at[k, zh],
            device_id=(j, other), device_id_type=MESH,
        )

    def grad_arrival(k, z_):
        return pltpu.make_async_remote_copy(
            src_ref=grad_s.at[0, 0], dst_ref=grad_r.at[k, z_ % 2, rows_of(z_)],
            send_sem=g_send.at[0, 0], recv_sem=g_recv.at[k, z_],
            device_id=at(zh_=z_, core_=k % 2, zl_=1 - zl), device_id_type=MESH,
        )

    def pext_copy(sc):
        return pltpu.make_async_remote_copy(
            src_ref=pext_s.at[sc], dst_ref=pext_r.at[member],
            send_sem=pe_send.at[sc], recv_sem=pe_recv.at[member],
            device_id=(KEEPERS[sc], other), device_id_type=MESH,
        )

    def pext_arrival(sc, j):
        return pltpu.make_async_remote_copy(
            src_ref=pext_s.at[sc], dst_ref=pext_r.at[j],
            send_sem=pe_send.at[sc], recv_sem=pe_recv.at[j],
            device_id=(j, other), device_id_type=MESH,
        )

    def gext_copy(sc, j):
        return pltpu.make_async_remote_copy(
            src_ref=gext_s.at[j], dst_ref=gext_r.at[sc],
            send_sem=ge_send.at[j], recv_sem=ge_recv.at[sc],
            device_id=(j, other), device_id_type=MESH,
        )

    def forward(sc):
        cols = pl.ds(sc * 2 * points, 2 * points)
        pre = po_v[:, cols] + dot(hh_v[...], adj_v[nodes : nodes + 2 * HALO, cols], 1, 0)
        sig = 0.5 * jnp.tanh(0.5 * pre) + 0.5
        h_v[:, cols] = (pre * sig).astype(BF16)
        f_v[:, cols] = sig * (1.0 + pre * (1.0 - sig))
        pred = dot(ow_t[...], h_v[:, cols], 1, 0)
        tails = []
        for b in range(GROUPS):
            block = pred[:, b * LANES : (b + 1) * LANES]
            pred_s[2 * sc + b // BLOCKS, b % BLOCKS] = block[:MAIN].astype(BF16)
            tails.append(block[MAIN : MAIN + EXTRA])
        pext_s[sc] = spread(tails).astype(BF16)
        for k in (2 * sc, 2 * sc + 1):
            for o in (1, 2, 0, 3):
                pred_copy(k, toward(o)).start()
        pext_copy(sc).start()

    def fair(preds, target, weight):
        out = [slope(p - target) * (1.0 / 8.0) for p in preds]
        pairs = [jnp.zeros(target.shape, F32) for _ in preds]
        for i in range(8):
            for j in range(i + 1, 8):
                s = slope(preds[i] - preds[j])
                pairs[i] = pairs[i] + s
                pairs[j] = pairs[j] - s
        return [weight * (o - q * (1.0 / 56.0)) for o, q in zip(out, pairs)]

    def pair_up(k):
        @pl.when(core == k % 2)
        def _():
            for j in range(8):
                pred_arrival(k, j).wait_recv()
            weight = coef_r[:, pl.ds(pl.multiple_of(k * points + (zh % 2) * LANES, LANES), LANES)]

            def tile(t, _):
                rows = pl.ds(pl.multiple_of(t * 16, 16), 16)
                target = tgt_r[k // 2, rows].astype(F32)
                grads = fair([pred_r[k // 2, j, rows].astype(F32) for j in range(8)], target, weight)
                for j in range(8):
                    grad_s[k // 2, j, rows] = grads[j].astype(BF16)
                return 0

            lax.fori_loop(0, ROWS // 16, tile, 0)
            for o in (1, 2, 0, 3):
                for c_ in range(2):
                    grad_copy(k, toward(o) * 2 + c_).start()

    def pair_up_tail(sc):
        keeper = KEEPERS[sc]

        @pl.when(member == keeper)
        def _():
            for j in range(8):
                pext_arrival(sc, j).wait_recv()
            weights = []
            for b in range(GROUPS):
                at_b = pl.ds((sc * GROUPS + b) * LANES, LANES)
                weights.append(jnp.broadcast_to(coef_r[:, at_b], (EXTRA, LANES)))
            grads = fair([pext_r[j].astype(F32) for j in range(8)], ttail_r[sc].astype(F32), spread(weights))
            for j in range(8):
                gext_s[j] = grads[j].astype(BF16)
            for j in range(8):
                gext_copy(sc, j).start()

    def backward(sc):
        cols = pl.ds(sc * 2 * points, 2 * points)
        for k in (2 * sc, 2 * sc + 1):
            for z_ in range(4):
                grad_arrival(k, z_).wait_recv()
        gext_copy(sc, 0).wait_recv()

        tail = gext_r[sc].astype(F32)
        blocks = []
        for b in range(GROUPS):
            mine = jnp.where(group == b, tail, 0.0).astype(BF16)
            main = grad_r[2 * sc + b // BLOCKS, b % BLOCKS]
            blocks.append(jnp.concatenate([main, mine, jnp.zeros((LANES - MAIN - EXTRA, LANES), BF16)], axis=0))
        gpred = jnp.concatenate(blocks, axis=1)
        dh = dot(ow_r[...], gpred, 1, 0)
        dpre_v[:, cols] = (dh * f_v[:, cols]).astype(BF16)
        gp_v[:, cols] = gpred

    forward(0)
    hear(0)
    tell(1)
    forward(1)
    for half in range(2):
        cols = pl.ds(half * 2 * points, 2 * points)
        x_v[:, cols] = (xo_v[:, cols] + dot(halo_v[...], adj_v[nodes : nodes + 2 * HALO, cols], 1, 0)).astype(BF16)
    for copy in lent:
        copy.wait_recv()
    sent.extend(lent)
    hear(1)
    tell(2)
    for k in range(CHUNKS):
        pair_up(k)
        if k % 2 == 1:
            pair_up_tail(k // 2)
    lead = 2 * LANES
    per_x, per_z, per_y = depth // nx, depth // (nx * nl), depth // (nx * nl * ny)

    def part(x_, core_):
        return pl.ds(pl.multiple_of(x_ * per_x + core_ * per_z, 8), per_z)

    hear(2)
    backward(0)
    early, late = pl.ds(0, 2 * points), pl.ds(2 * points, 2 * points)
    gw_v[:, 0:depth] = dot(x_v[:, early], dpre_v[:, early], 1, 1)
    gw_v[:, depth:width] = dot(h_v[:, early], gp_v[:, early], 1, 1)
    backward(1)
    gw_v[:, 0:lead] += dot(x_v[:, late], dpre_v[0:lead, late], 1, 1)
    for x_ in range(nx):
        b0_s[x_] = gw_v[part(x_, 1 - core), 0:lead].astype(BF16)
    b0 = remote(b0_s, b0_r, s0_sem, 0, at(core_=1 - core))
    b0.start()
    gw_v[:, lead:depth] += dot(x_v[:, late], dpre_v[lead:depth, late], 1, 1)
    gw_v[:, depth:width] += dot(h_v[:, late], gp_v[:, late], 1, 1)
    for x_ in range(nx):
        a0_s[x_] = gw_v[part(x_, 1 - core), lead:width].astype(BF16)
    a0 = remote(a0_s, a0_r, s0_sem, 1, at(core_=1 - core))
    a0.start()
    sent.extend([b0, a0])

    b0.wait_recv()
    for x_ in range(nx):
        total = gw_v[part(x_, core), 0:lead] + b0_r[x_].astype(F32)
        for y_ in range(ny):
            b1_f[y_, x_ * per_y : (x_ + 1) * per_y] = total[y_ * per_y : (y_ + 1) * per_y]
    b1 = []
    for s in (4, 3, 5, 2, 6, 1, 7):
        if s < ny:
            y_ = (yi + s * turn) % ny
            b1_s[y_] = b1_f[y_].astype(BF16)
            copy = remote(b1_s.at[y_], b1_r.at[s - 1], b1_sem, s - 1, at(y_=y_))
            copy.start()
            b1.append(copy)
    a0.wait_recv()
    for x_ in range(nx):
        a1_f[x_] = gw_v[part(x_, core), lead:width] + a0_r[x_].astype(F32)
    a1 = []
    for s in (2, 1, 3):
        if s < nx:
            x_ = (xi + s * (1 + (nx - 2) * core)) % nx
            a1_s[x_] = a1_f[x_].astype(BF16)
            copy = remote(a1_s.at[x_], a1_r.at[s - 1], a1_sem, s - 1, at(x_=x_))
            copy.start()
            a1.append(copy)
    sent.extend(a1 + b1)

    for half in range(2):
        cols = pl.ds(half * 2 * points, 2 * points)
        dx_v[:, cols] = dot(hw_v[...], dpre_v[:, cols], 1, 0).astype(BF16)
    down, up = pack(dot(dx_v[...], adj_v[nodes : nodes + 2 * HALO], 1, 1))
    ghalo_s[0] = down.astype(BF16)
    ghalo_s[1] = up.astype(BF16)
    ghalo_down = remote(ghalo_s.at[0], ghalo_r.at[0], ghalo_sem, 0, below)
    ghalo_up = remote(ghalo_s.at[1], ghalo_r.at[1], ghalo_sem, 1, above)
    ghalo_down.start()
    ghalo_up.start()
    sent.extend([ghalo_down, ghalo_up])
    eg_v[...] = dot(dx_v[...], adj_v[0:nodes], 1, 1)
    halos_left()
    points_left()

    for copy in a1:
        copy.wait_recv()
    total = a1_f[xi]
    for s in range(nx - 1):
        total = total + a1_r[s].astype(F32)
    for y_ in range(ny):
        rows = total[y_ * per_y : (y_ + 1) * per_y]
        rest = jnp.concatenate([rows[:, lead:], jnp.zeros((per_y, LANES), F32)], axis=1)
        a2_f[y_] = jnp.concatenate([rows[:, :lead], rest], axis=0)
        a2_s[y_] = a2_f[y_].astype(BF16)
    a2 = []
    for s in (4, 3, 5, 2, 6, 1, 7):
        if s < ny:
            y_ = (yi + s * turn) % ny
            copy = remote(a2_s.at[y_], a2_r.at[s - 1], a2_sem, s - 1, at(y_=y_))
            copy.start()
            a2.append(copy)
    for copy in b1:
        copy.wait_recv()
    total = b1_f[yi]
    for s in range(ny - 1):
        total = total + b1_r[s].astype(F32)
    for x_ in range(nx):
        rows = total[x_ * per_y : (x_ + 1) * per_y]
        b2_f[x_] = jnp.concatenate([rows[:, :LANES], rows[:, LANES:]], axis=0)
        b2_s[x_] = b2_f[x_].astype(BF16)
    b2 = []
    for s in (2, 1, 3):
        if s < nx:
            x_ = (xi + s * (1 + (nx - 2) * core)) % nx
            copy = remote(b2_s.at[x_], b2_r.at[s - 1], b2_sem, s - 1, at(x_=x_))
            copy.start()
            b2.append(copy)
    sent_left()
    sent.extend(a2 + b2)

    ghalo_down.wait_recv()
    ghalo_up.wait_recv()
    top, bottom = unpack(ghalo_r[1].astype(F32), ghalo_r[0].astype(F32))
    gm_out[0, 0 : depth // 2] = eg_v[0 : depth // 2] + top
    gm_out[0, depth // 2 : depth] = eg_v[depth // 2 : depth] + bottom

    for copy in b2:
        copy.wait_recv()
    total = b2_f[xi]
    for s in range(nx - 1):
        total = total + b2_r[s].astype(F32)
    s3_s[:, 0:LANES] = total.astype(BF16)
    for copy in a2:
        copy.wait_recv()
    total = a2_f[yi]
    for s in range(ny - 1):
        total = total + a2_r[s].astype(F32)
    s3_s[:, LANES : 3 * LANES] = total.astype(BF16)
    here = zh * nl + zl

    def s3_copy(z_, c_, slot):
        return pltpu.make_async_remote_copy(
            src_ref=s3_s, dst_ref=s3_r.at[slot],
            send_sem=s3_send.at[z_ * 2 + c_], recv_sem=s3_recv.at[slot],
            device_id=at(zh_=z_, core_=c_, zl_=core), device_id_type=MESH,
        )

    for a in (2, 1, 3):
        for c_ in range(2):
            s3_copy((zh + a) % 4, c_, here).start()
    for c_ in range(2):
        mine = (zl == core) & (core == c_)

        @pl.when(jnp.logical_not(mine))
        def _():
            s3_copy(zh, c_, here).start()

        @pl.when(mine)
        def _():
            s3_r[here] = s3_s[...]

    sent_left()
    for a in range(4):
        for l_ in range(nl):
            arrival = s3_copy(0, 0, (zh + a) % 4 * nl + l_)
            if a == 0:
                pl.when(jnp.logical_not((l_ == zl) & (core == zl)))(arrival.wait_recv)
            else:
                arrival.wait_recv()

    total = s3_r[0].astype(F32)
    for z_ in range(1, 4 * nl):
        total = total + s3_r[z_].astype(F32)
    gh_out[:, 0:LANES] = total[:per_y, 0:LANES]
    gh_out[:, LANES:lead] = total[per_y:, 0:LANES]
    gh_out[:, lead:depth] = total[:per_y, LANES : LANES + depth - lead]
    second = total[per_y:, LANES : 2 * LANES]
    lane = lax.broadcasted_iota(jnp.int32, second.shape, 1)
    tail = jnp.where((lane >= MAIN) & (lane < MAIN + EXTRA), second, 0.0)
    folded = tail
    for b in range(1, GROUPS):
        folded = folded + pltpu.roll(tail, LANES - 4 * b, 1)
    go_out[...] = jnp.where(lane < MAIN, second, folded)[:, : go_out.shape[1]]
    last_left()


def flush(gh_in, go_in, gm_in, gh_out, go_out, gm_out, sem):
    copies = [pltpu.make_async_copy(a, b, sem.at[i]) for i, (a, b) in enumerate(((gm_in, gm_out), (gh_in, gh_out), (go_in, go_out)))]
    for copy in copies:
        copy.start()
    for copy in copies:
        copy.wait()


def solution(mesh, dims=(4, 2, 8)):
    def local(mesh_latent, grid_latent, edge_sources, edge_weights, area_weight, band_counts, target, hidden_weight, out_weight):
        nx, nl, ny = dims
        _, depth, nodes = mesh_latent.shape
        points = grid_latent.shape[2]
        variables = target.shape[0]
        per_x, per_z, per_y = depth // nx, depth // (nx * nl), depth // (nx * nl * ny)
        width, lead = depth + LANES, 2 * LANES
        tall = width - lead
        area = area_weight.reshape(1, points)
        vm, dma = pltpu.VMEM, pltpu.SemaphoreType.DMA
        scratch = [
            vm((depth, nodes), BF16), vm((depth, points), BF16), vm((3, points), jnp.int32), vm((3, points), BF16),
            vm((1, points), F32), vm((1, 1), jnp.int32), vm((variables, points), BF16), vm((depth, depth), BF16), vm((variables, depth), BF16),
            vm((104, points), F32), vm((1, points), F32), vm((depth, depth), BF16), vm((LANES, depth), F32), vm((depth, LANES), BF16), vm((LANES, depth), BF16),
            vm((depth, 2 * HALO), BF16), vm((depth, 2 * HALO), BF16), vm((depth, points), F32), vm((depth, points), F32),
            vm((nodes + 2 * HALO, points), BF16), vm((depth, points), BF16), vm((depth, points), BF16), vm((depth, points), F32),
            vm((2, depth // 2, LANES), BF16), vm((2, depth // 2, LANES), BF16), vm((2, depth // 2, LANES), BF16), vm((2, depth // 2, LANES), BF16),
            vm((CHUNKS, BLOCKS, MAIN, LANES), BF16), vm((2, EXTRA, LANES), BF16), vm((2, 8, ROWS, LANES), BF16), vm((8, EXTRA, LANES), BF16),
            vm((2, 8, ROWS, LANES), BF16), vm((8, EXTRA, LANES), BF16), vm((CHUNKS, BLOCKS, MAIN, LANES), BF16), vm((2, EXTRA, LANES), BF16),
            vm((depth, width), F32), vm((depth, nodes), F32), vm((depth, points), BF16), vm((depth, points), BF16), vm((LANES, points), BF16),
            vm((nx, per_z, tall), BF16), vm((nx, per_z, tall), BF16), vm((nx, per_z, lead), BF16), vm((nx, per_z, lead), BF16),
            vm((nx, per_z, tall), F32), vm((nx, per_z, tall), BF16), vm((nx - 1, per_z, tall), BF16),
            vm((ny, nx * per_y, lead), F32), vm((ny, nx * per_y, lead), BF16), vm((ny - 1, nx * per_y, lead), BF16),
            vm((ny, 2 * per_y, lead), F32), vm((ny, 2 * per_y, lead), BF16), vm((ny - 1, 2 * per_y, lead), BF16),
            vm((nx, 2 * per_y, LANES), F32), vm((nx, 2 * per_y, LANES), BF16), vm((nx - 1, 2 * per_y, LANES), BF16),
            vm((2 * per_y, 3 * LANES), BF16), vm((4 * nl, 2 * per_y, 3 * LANES), BF16),
            pltpu.SemaphoreType.REGULAR((3,)),
            vm((1, points), F32), vm((2, EXTRA, LANES), BF16), vm((2, EXTRA, LANES), BF16), vm((2, ROWS, LANES), BF16), dma((2, 4)),
            dma((9,)), dma((2, 2)), dma((2, 2)), dma((CHUNKS, 4)), dma((2, 8)), dma((2,)), dma((8,)),
            dma((2, 8)), dma((CHUNKS, 4)), dma((8,)), dma((2,)),
            dma((2, 2)), dma((2, nx - 1)), dma((2, ny - 1)), dma((2, ny - 1)), dma((2, nx - 1)), dma((8,)), dma((4 * nl,)),
        ]
        sums = pl.pallas_call(
            functools.partial(kernel, dims),
            out_shape=(
                pltpu.VMEM((per_y, depth), F32),
                pltpu.VMEM((per_y, variables), F32),
                pltpu.VMEM((1, depth, nodes), F32),
            ),
            in_specs=[pl.BlockSpec(memory_space=pl.ANY)] * 9,
            out_specs=[pl.BlockSpec(memory_space=pltpu.VMEM)] * 3,
            scratch_shapes=scratch,
            compiler_params=pltpu.CompilerParams(
                collective_id=0, has_side_effects=True, vmem_limit_bytes=62 * 1024 * 1024
            ),
            name="step",
        )(mesh_latent, grid_latent, edge_sources, edge_weights, area, band_counts.reshape(1, 1), target, hidden_weight, out_weight.T)
        return pl.pallas_call(
            flush,
            out_shape=tuple(jax.ShapeDtypeStruct(a.shape, F32) for a in sums),
            in_specs=[pl.BlockSpec(memory_space=pl.ANY)] * 3,
            out_specs=[pl.BlockSpec(memory_space=pl.ANY)] * 3,
            scratch_shapes=[dma((3,))],
            compiler_params=pltpu.CompilerParams(vmem_limit_bytes=1024 * 1024),
            name="flush",
        )(*sums)

    return jax.shard_map(
        local,
        mesh=mesh,
        in_specs=(
            P("member", None, "grid"),
            P("member", None, "grid"),
            P(None, "grid"),
            P(None, "grid"),
            P("grid"),
            P("grid"),
            P(None, "grid"),
            P(),
            P(),
        ),
        out_specs=(P("grid", None), P("grid", None), P("member", None, "grid")),
        check_vma=False,
    )
```

```python
import functools

import jax
import jax.numpy as jnp
from jax import lax
from jax.experimental import pallas as pl
from jax.experimental.pallas import tpu as pltpu
from jax.sharding import PartitionSpec as P

HALO = 64
LANES = 128
CHUNKS = 4
BLOCKS = 2
GROUPS = 4
KEEPERS = (4, 6)
ROWS = 48
MAIN = 96
EXTRA = 16
MESH = pl.DeviceIdType.MESH

smooth_sq = 0.01
loss_scale = 4096.0

F32 = jnp.float32
BF16 = jnp.bfloat16


def slope(diff):
    return diff * lax.rsqrt(diff * diff + smooth_sq)


def dot(a, b, da, db):
    return lax.dot_general(a, b, (((da,), (db,)), ((), ())), preferred_element_type=F32)


def low_lanes(shape):
    return lax.broadcasted_iota(jnp.int32, shape, 1) < HALO


def pack(tile):
    half = tile.shape[0] // 2
    top, bottom = tile[:half], tile[half:]
    low = low_lanes(top.shape)
    down = jnp.where(low, top, pltpu.roll(bottom, HALO, 1))
    up = jnp.where(low, pltpu.roll(top, HALO, 1), bottom)
    return down, up


def unpack(below, above):
    low = low_lanes(below.shape)
    top = jnp.where(low, below, pltpu.roll(above, HALO, 1))
    bottom = jnp.where(low, pltpu.roll(below, HALO, 1), above)
    return top, bottom


def kernel(
    dims,
    mesh_in, grid_in, src_in, wgt_in, area_in, count_in, target_in, hw_in, ow_in,
    gh_out, go_out, gm_out,
    mesh_v, grid_v, src_v, wgt_v, area_v, count_v, tgt_v, hw_v, ow_v,
    tgt_f, coef_v, hw_t, ow_f, ow_r, ow_t, halo_v, hh_v, xo_v, po_v, adj_v, x_v, h_v, f_v,
    halo_s, halo_r, ghalo_s, ghalo_r,
    pred_s, pext_s, pred_r, pext_r, grad_s, grad_r,
    gw_v, eg_v, dpre_v, dx_v, gp_v, a0_s, a0_r, b0_s, b0_r, a1_f, a1_s, a1_r, b1_f, b1_s, b1_r, a2_f, a2_s, a2_r, b2_f, b2_s, b2_r, s3_s, s3_r,
    near_sem, coef_r, ttail_s, ttail_r, tgt_r, t_sem, load_sem, halo_sem, ghalo_sem, p_send, p_recv, pe_send, pe_recv, g_send, g_recv,
    s0_sem, a1_sem, b1_sem, a2_sem, b2_sem, s3_send, s3_recv,
):
    nx, nl, ny = dims
    nodes = mesh_v.shape[1]
    depth = hw_v.shape[0]
    width = depth + LANES
    points = grid_v.shape[1] // CHUNKS
    member, band = lax.axis_index("member"), lax.axis_index("grid")
    zh, core = member // 2, member % 2
    xi, zl, yi = band // (nl * ny), (band // ny) % nl, band % ny
    bands = nx * nl * ny

    def at(zh_=None, core_=None, x_=None, zl_=None, y_=None):
        zh_ = zh if zh_ is None else zh_
        core_ = core if core_ is None else core_
        x_ = xi if x_ is None else x_
        zl_ = zl if zl_ is None else zl_
        y_ = yi if y_ is None else y_
        return (zh_ * 2 + core_, x_ * (nl * ny) + zl_ * ny + y_)

    above = (member, (band + 1) % bands)
    below = (member, (band + bands - 1) % bands)

    def remote(src, dst, sems, i, device):
        return pltpu.make_async_remote_copy(
            src_ref=src, dst_ref=dst, send_sem=sems.at[0, i], recv_sem=sems.at[1, i],
            device_id=device, device_id_type=MESH,
        )

    barrier = pltpu.get_barrier_semaphore()
    other = xi * (nl * ny) + (1 - zl) * ny + yi
    column = [(a, b, c) for a in (2, 1, 3, 0) for b in range(2) for c in range(nl) if (a, b, c) != (0, 0, 0)]
    beside = [at(y_=(yi + 1) % ny), at(y_=(yi + ny - 1) % ny), at(x_=(xi + 1) % nx), at(x_=(xi + nx - 1) % nx)]
    partners = [at(zh_=(zh + a) % 4, core_=(core + b) % 2, zl_=(zl + c) % nl) for a, b, c in column[:4]]
    partners += [above, below] + beside
    partners += [at(zh_=(zh + a) % 4, core_=(core + b) % 2, zl_=(zl + c) % nl) for a, b, c in column[4:]]

    def tell(i):
        for partner in beside if i == 0 else beside[:2]:
            pl.semaphore_signal(near_sem.at[i], inc=1, device_id=partner, device_id_type=MESH)

    def hear(i):
        pl.semaphore_wait(near_sem.at[i], 4 if i == 0 else 2)

    def load(i, src, dst):
        copy = pltpu.make_async_copy(src, dst, load_sem.at[i])
        copy.start()
        return copy

    load_mesh = load(0, mesh_in.at[0], mesh_v)
    for partner in partners:
        pl.semaphore_signal(barrier, inc=1, device_id=partner, device_id_type=MESH)
    load_src = load(1, src_in, src_v)
    load_wgt = load(2, wgt_in, wgt_v)
    load_hw = load(3, hw_in, hw_v)
    load_ow = load(4, ow_in, ow_v)
    load_grid = load(5, grid_in.at[0], grid_v)
    load_area = load(6, area_in, area_v)
    load_tgt = load(7, target_in, tgt_v)
    load_count = load(8, count_in, count_v)

    load_mesh.wait()
    down, up = pack(mesh_v[...].astype(F32))
    halo_s[0] = down.astype(BF16)
    halo_s[1] = up.astype(BF16)
    pl.semaphore_wait(barrier, len(partners))
    halo_down = remote(halo_s.at[0], halo_r.at[0], halo_sem, 0, below)
    halo_up = remote(halo_s.at[1], halo_r.at[1], halo_sem, 1, above)
    halo_down.start()
    halo_up.start()
    tell(0)


    load_hw.wait()
    hw_t[...] = hw_v[...].astype(F32).T.astype(BF16)
    load_ow.wait()
    count = ow_v.shape[0]
    ow_f[MAIN:LANES] = jnp.zeros((LANES - MAIN, depth), F32)
    ow_f[0:count] = ow_v[...].astype(F32)
    tail = ow_f[MAIN : MAIN + 8]
    tail = tail + pltpu.roll(tail, 4, 0)
    ow_f[MAIN : MAIN + 8] = tail
    ow_f[MAIN + 8 : MAIN + 16] = tail
    ow_t[...] = ow_f[...].astype(BF16)
    ow_r[...] = ow_f[...].T.astype(BF16)

    load_src.wait()
    load_wgt.wait()
    row = lax.broadcasted_iota(jnp.int32, (nodes + 2 * HALO, points), 0)
    slot = jnp.where(row < nodes, row, jnp.where(row < nodes + HALO, row - (nodes + HALO), row - HALO))
    for chunk in range(CHUNKS):
        cols = pl.ds(chunk * points, points)
        adj = jnp.zeros(row.shape, F32)
        for k in range(3):
            source = src_v[pl.ds(k, 1), cols] - band * nodes
            weight = wgt_v[:, cols].astype(F32)[k : k + 1]
            adj = jnp.where(source == slot, weight, adj)
        adj_v[:, cols] = adj.astype(BF16)

    load_tgt.wait()
    tgt_f[0 : tgt_v.shape[0]] = tgt_v[...].astype(F32)
    load_area.wait()
    load_count.wait()
    place = lax.broadcasted_iota(jnp.int32, (1, CHUNKS * points), 1)
    live = (place < count_v[...]).astype(F32)
    coef_v[...] = loss_scale * area_v[...] * live / tgt_v.shape[0]
    group = lax.broadcasted_iota(jnp.int32, (EXTRA, LANES), 0) // 4

    def spread(blocks):
        out = blocks[0]
        for b in range(1, GROUPS):
            out = jnp.where(group == b, blocks[b], out)
        return out

    def rows_of(z_):
        return pl.ds(pl.multiple_of(ROWS * (z_ // 2), 16), ROWS)

    row8 = lax.broadcasted_iota(jnp.int32, (8, LANES), 0)
    for sc in range(2):
        targets = []
        for b in range(GROUPS):
            tail = tgt_f[MAIN : MAIN + 8, pl.ds((sc * GROUPS + b) * LANES, LANES)]
            tail = jnp.where(row8 < 4, tail, pltpu.roll(tail, 4, 0))
            targets.append(jnp.concatenate([tail, tail], axis=0))
        ttail_s[sc] = spread(targets).astype(BF16)
    mate = at(zl_=1 - zl)
    lent = [remote(coef_v, coef_r, t_sem, 0, mate), remote(ttail_s, ttail_r, t_sem, 1, mate)]
    for i in range(2):
        lanes = pl.ds(pl.multiple_of((2 * i + core) * points + (zh % 2) * LANES, LANES), LANES)
        lent.append(remote(tgt_v.at[rows_of(zh), lanes], tgt_r.at[i], t_sem, 2 + i, mate))
    for copy in lent:
        copy.start()

    turn = 1 + (ny - 2) * core
    sent = []

    def halos_left():
        halo_down.wait_send()
        halo_up.wait_send()

    def points_left():
        for k in range(CHUNKS):
            for z_ in range(4):
                pred_copy(k, z_).wait_send()
            pl.when(core == k % 2)(functools.partial(left_grad, k))
        for sc in range(2):
            pext_copy(sc).wait_send()

    def sent_left():
        for copy in sent:
            copy.wait_send()
        sent.clear()

    def last_left():
        for a in range(4):
            for c_ in range(2):
                left = s3_copy((zh + a) % 4, c_, here)
                if a == 0:
                    pl.when(jnp.logical_not((zl == core) & (core == c_)))(left.wait_send)
                else:
                    left.wait_send()

    def left_grad(k):
        def left(rows):
            for j in range(8):
                grad_copy(k, j, rows).wait_send()

        if k % 2 == 0:
            pl.when(member == KEEPERS[k // 2])(functools.partial(left, ROWS + EXTRA))
            pl.when(member != KEEPERS[k // 2])(functools.partial(left, ROWS))
        else:
            left(ROWS)

    load_grid.wait()
    for half in range(2):
        cols = pl.ds(half * 2 * points, 2 * points)
        xo_v[:, cols] = dot(mesh_v[...], adj_v[0:nodes, cols], 1, 0) + grid_v[:, cols].astype(F32)
        po_v[:, cols] = dot(hw_t[...], xo_v[:, cols].astype(BF16), 1, 0)
    halo_down.wait_recv()
    halo_up.wait_recv()
    top, bottom = unpack(halo_r[1].astype(F32), halo_r[0].astype(F32))
    halo_v[0 : depth // 2] = top.astype(BF16)
    halo_v[depth // 2 : depth] = bottom.astype(BF16)
    hh_v[...] = dot(hw_t[...], halo_v[...], 1, 0).astype(BF16)

    def toward(o):
        return (zh + zl + o + core * (3 - 2 * o)) % 4

    def pred_copy(k, z_):
        return pltpu.make_async_remote_copy(
            src_ref=pred_s.at[k, z_ % 2, rows_of(z_)], dst_ref=pred_r.at[k // 2, member],
            send_sem=p_send.at[k, z_], recv_sem=p_recv.at[k // 2, member],
            device_id=at(zh_=z_, core_=k % 2, zl_=1 - zl), device_id_type=MESH,
        )

    def pred_arrival(k, j):
        return pltpu.make_async_remote_copy(
            src_ref=pred_s.at[k, 0, pl.ds(0, ROWS)], dst_ref=pred_r.at[k // 2, j],
            send_sem=p_send.at[k, 0], recv_sem=p_recv.at[k // 2, j],
            device_id=(j, other), device_id_type=MESH,
        )

    def grad_copy(k, j, rows):
        return pltpu.make_async_remote_copy(
            src_ref=grad_s.at[k // 2, j, pl.ds(0, rows)], dst_ref=grad_r.at[k, zh, pl.ds(0, rows)],
            send_sem=g_send.at[k // 2, j], recv_sem=g_recv.at[k, zh],
            device_id=(j, other), device_id_type=MESH,
        )

    def grad_arrival(k, z_):
        rows = ROWS + EXTRA if 2 * z_ + k % 2 == KEEPERS[k // 2] else ROWS
        return pltpu.make_async_remote_copy(
            src_ref=grad_s.at[0, 0, pl.ds(0, rows)], dst_ref=grad_r.at[k, z_, pl.ds(0, rows)],
            send_sem=g_send.at[0, 0], recv_sem=g_recv.at[k, z_],
            device_id=at(zh_=z_, core_=k % 2, zl_=1 - zl), device_id_type=MESH,
        )

    def pext_copy(sc):
        return pltpu.make_async_remote_copy(
            src_ref=pext_s.at[sc], dst_ref=pext_r.at[member],
            send_sem=pe_send.at[sc], recv_sem=pe_recv.at[member],
            device_id=(KEEPERS[sc], other), device_id_type=MESH,
        )

    def pext_arrival(sc, j):
        return pltpu.make_async_remote_copy(
            src_ref=pext_s.at[sc], dst_ref=pext_r.at[j],
            send_sem=pe_send.at[sc], recv_sem=pe_recv.at[j],
            device_id=(j, other), device_id_type=MESH,
        )

    def forward(sc):
        cols = pl.ds(sc * 2 * points, 2 * points)
        pre = po_v[:, cols] + dot(hh_v[...], adj_v[nodes : nodes + 2 * HALO, cols], 1, 0)
        sig = 0.5 * jnp.tanh(0.5 * pre) + 0.5
        h_v[:, cols] = (pre * sig).astype(BF16)
        f_v[:, cols] = sig * (1.0 + pre * (1.0 - sig))
        pred = dot(ow_t[...], h_v[:, cols], 1, 0)
        tails = []
        for b in range(GROUPS):
            block = pred[:, b * LANES : (b + 1) * LANES]
            pred_s[2 * sc + b // BLOCKS, b % BLOCKS] = block[:MAIN].astype(BF16)
            tails.append(block[MAIN : MAIN + EXTRA])
        pext_s[sc] = spread(tails).astype(BF16)
        for k in (2 * sc, 2 * sc + 1):
            for o in (1, 2, 0, 3):
                pred_copy(k, toward(o)).start()
        pext_copy(sc).start()

    def fair(preds, target, weight):
        out = [slope(p - target) * (1.0 / 8.0) for p in preds]
        pairs = [jnp.zeros(target.shape, F32) for _ in preds]
        for i in range(8):
            for j in range(i + 1, 8):
                s = slope(preds[i] - preds[j])
                pairs[i] = pairs[i] + s
                pairs[j] = pairs[j] - s
        return [weight * (o - q * (1.0 / 56.0)) for o, q in zip(out, pairs)]

    def pair_up(k):
        @pl.when(core == k % 2)
        def _():
            for j in range(8):
                pred_arrival(k, j).wait_recv()
            weight = coef_r[:, pl.ds(pl.multiple_of(k * points + (zh % 2) * LANES, LANES), LANES)]

            def tile(t, _):
                rows = pl.ds(pl.multiple_of(t * 16, 16), 16)
                target = tgt_r[k // 2, rows].astype(F32)
                grads = fair([pred_r[k // 2, j, rows].astype(F32) for j in range(8)], target, weight)
                for j in range(8):
                    grad_s[k // 2, j, rows] = grads[j].astype(BF16)
                return 0

            lax.fori_loop(0, ROWS // 16, tile, 0)
            def send(rows):
                for o in (1, 2, 0, 3):
                    for c_ in range(2):
                        grad_copy(k, toward(o) * 2 + c_, rows).start()

            if k % 2 == 0:
                keeper = KEEPERS[k // 2]

                @pl.when(member == keeper)
                def _():
                    pair_up_tail(k // 2)
                    send(ROWS + EXTRA)

                pl.when(member != keeper)(functools.partial(send, ROWS))
            else:
                send(ROWS)

    def pair_up_tail(sc):
        for j in range(8):
            pext_arrival(sc, j).wait_recv()
        weights = []
        for b in range(GROUPS):
            at_b = pl.ds((sc * GROUPS + b) * LANES, LANES)
            weights.append(jnp.broadcast_to(coef_r[:, at_b], (EXTRA, LANES)))
        grads = fair([pext_r[j].astype(F32) for j in range(8)], ttail_r[sc].astype(F32), spread(weights))
        for j in range(8):
            grad_s[sc, j, ROWS : ROWS + EXTRA] = grads[j].astype(BF16)

    def backward(sc):
        cols = pl.ds(sc * 2 * points, 2 * points)
        for k in (2 * sc, 2 * sc + 1):
            for z_ in range(4):
                grad_arrival(k, z_).wait_recv()

        tail = grad_r[2 * sc, KEEPERS[sc] // 2, ROWS : ROWS + EXTRA].astype(F32)
        blocks = []
        for b in range(GROUPS):
            mine = jnp.where(group == b, tail, 0.0).astype(BF16)
            main = [grad_r[2 * sc + b // BLOCKS, b % BLOCKS + 2 * i, 0:ROWS] for i in range(2)]
            blocks.append(jnp.concatenate([*main, mine, jnp.zeros((LANES - MAIN - EXTRA, LANES), BF16)], axis=0))
        gpred = jnp.concatenate(blocks, axis=1)
        dh = dot(ow_r[...], gpred, 1, 0)
        dpre_v[:, cols] = (dh * f_v[:, cols]).astype(BF16)
        gp_v[:, cols] = gpred

    forward(0)
    hear(0)
    tell(1)
    forward(1)
    for half in range(2):
        cols = pl.ds(half * 2 * points, 2 * points)
        x_v[:, cols] = (xo_v[:, cols] + dot(halo_v[...], adj_v[nodes : nodes + 2 * HALO, cols], 1, 0)).astype(BF16)
    for copy in lent:
        copy.wait_recv()
    sent.extend(lent)
    hear(1)
    tell(2)
    for k in range(CHUNKS):
        pair_up(k)
    lead = 2 * LANES
    per_x, per_z, per_y = depth // nx, depth // (nx * nl), depth // (nx * nl * ny)

    def part(x_, core_):
        return pl.ds(pl.multiple_of(x_ * per_x + core_ * per_z, 8), per_z)

    hear(2)
    backward(0)
    early, late = pl.ds(0, 2 * points), pl.ds(2 * points, 2 * points)
    gw_v[:, 0:depth] = dot(x_v[:, early], dpre_v[:, early], 1, 1)
    gw_v[:, depth:width] = dot(h_v[:, early], gp_v[:, early], 1, 1)
    backward(1)
    gw_v[:, 0:lead] += dot(x_v[:, late], dpre_v[0:lead, late], 1, 1)
    for x_ in range(nx):
        b0_s[x_] = gw_v[part(x_, 1 - core), 0:lead].astype(BF16)
    b0 = remote(b0_s, b0_r, s0_sem, 0, at(core_=1 - core))
    b0.start()
    gw_v[:, lead:depth] += dot(x_v[:, late], dpre_v[lead:depth, late], 1, 1)
    gw_v[:, depth:width] += dot(h_v[:, late], gp_v[:, late], 1, 1)
    for x_ in range(nx):
        a0_s[x_] = gw_v[part(x_, 1 - core), lead:width].astype(BF16)
    a0 = remote(a0_s, a0_r, s0_sem, 1, at(core_=1 - core))
    a0.start()
    sent.extend([b0, a0])

    b0.wait_recv()
    for x_ in range(nx):
        total = gw_v[part(x_, core), 0:lead] + b0_r[x_].astype(F32)
        for y_ in range(ny):
            b1_f[y_, x_ * per_y : (x_ + 1) * per_y] = total[y_ * per_y : (y_ + 1) * per_y]
    b1 = []
    for s in (4, 3, 5, 2, 6, 1, 7):
        if s < ny:
            y_ = (yi + s * turn) % ny
            b1_s[y_] = b1_f[y_].astype(BF16)
            copy = remote(b1_s.at[y_], b1_r.at[s - 1], b1_sem, s - 1, at(y_=y_))
            copy.start()
            b1.append(copy)
    a0.wait_recv()
    for x_ in range(nx):
        a1_f[x_] = gw_v[part(x_, core), lead:width] + a0_r[x_].astype(F32)
    a1 = []
    for s in (2, 1, 3):
        if s < nx:
            x_ = (xi + s * (1 + (nx - 2) * core)) % nx
            a1_s[x_] = a1_f[x_].astype(BF16)
            copy = remote(a1_s.at[x_], a1_r.at[s - 1], a1_sem, s - 1, at(x_=x_))
            copy.start()
            a1.append(copy)
    sent.extend(a1 + b1)

    for half in range(2):
        cols = pl.ds(half * 2 * points, 2 * points)
        dx_v[:, cols] = dot(hw_v[...], dpre_v[:, cols], 1, 0).astype(BF16)
    down, up = pack(dot(dx_v[...], adj_v[nodes : nodes + 2 * HALO], 1, 1))
    ghalo_s[0] = down.astype(BF16)
    ghalo_s[1] = up.astype(BF16)
    ghalo_down = remote(ghalo_s.at[0], ghalo_r.at[0], ghalo_sem, 0, below)
    ghalo_up = remote(ghalo_s.at[1], ghalo_r.at[1], ghalo_sem, 1, above)
    ghalo_down.start()
    ghalo_up.start()
    sent.extend([ghalo_down, ghalo_up])
    eg_v[...] = dot(dx_v[...], adj_v[0:nodes], 1, 1)
    halos_left()
    points_left()

    for copy in a1:
        copy.wait_recv()
    total = a1_f[xi]
    for s in range(nx - 1):
        total = total + a1_r[s].astype(F32)
    for y_ in range(ny):
        rows = total[y_ * per_y : (y_ + 1) * per_y]
        rest = jnp.concatenate([rows[:, lead:], jnp.zeros((per_y, LANES), F32)], axis=1)
        a2_f[y_] = jnp.concatenate([rows[:, :lead], rest], axis=0)
        a2_s[y_] = a2_f[y_].astype(BF16)
    a2 = []
    for s in (4, 3, 5, 2, 6, 1, 7):
        if s < ny:
            y_ = (yi + s * turn) % ny
            copy = remote(a2_s.at[y_], a2_r.at[s - 1], a2_sem, s - 1, at(y_=y_))
            copy.start()
            a2.append(copy)
    for copy in b1:
        copy.wait_recv()
    total = b1_f[yi]
    for s in range(ny - 1):
        total = total + b1_r[s].astype(F32)
    for x_ in range(nx):
        rows = total[x_ * per_y : (x_ + 1) * per_y]
        b2_f[x_] = jnp.concatenate([rows[:, :LANES], rows[:, LANES:]], axis=0)
        b2_s[x_] = b2_f[x_].astype(BF16)
    b2 = []
    for s in (2, 1, 3):
        if s < nx:
            x_ = (xi + s * (1 + (nx - 2) * core)) % nx
            copy = remote(b2_s.at[x_], b2_r.at[s - 1], b2_sem, s - 1, at(x_=x_))
            copy.start()
            b2.append(copy)
    sent_left()
    sent.extend(a2 + b2)

    ghalo_down.wait_recv()
    ghalo_up.wait_recv()
    top, bottom = unpack(ghalo_r[1].astype(F32), ghalo_r[0].astype(F32))
    gm_out[0, 0 : depth // 2] = eg_v[0 : depth // 2] + top
    gm_out[0, depth // 2 : depth] = eg_v[depth // 2 : depth] + bottom

    for copy in b2:
        copy.wait_recv()
    total = b2_f[xi]
    for s in range(nx - 1):
        total = total + b2_r[s].astype(F32)
    s3_s[:, 0:LANES] = total.astype(BF16)
    for copy in a2:
        copy.wait_recv()
    total = a2_f[yi]
    for s in range(ny - 1):
        total = total + a2_r[s].astype(F32)
    s3_s[:, LANES : 3 * LANES] = total.astype(BF16)
    here = zh * nl + zl

    def s3_copy(z_, c_, slot):
        return pltpu.make_async_remote_copy(
            src_ref=s3_s, dst_ref=s3_r.at[slot],
            send_sem=s3_send.at[z_ * 2 + c_], recv_sem=s3_recv.at[slot],
            device_id=at(zh_=z_, core_=c_, zl_=core), device_id_type=MESH,
        )

    for z_ in range(4):
        for c_ in range(2):
            mine = (zh == z_) & (zl == core) & (core == c_)
            pl.when(jnp.logical_not(mine))(s3_copy(z_, c_, here).start)

            @pl.when(mine)
            def _():
                s3_r[here] = s3_s[...]

    sent_left()
    for a in range(4):
        for l_ in range(nl):
            arrival = s3_copy(0, 0, (zh + a) % 4 * nl + l_)
            if a == 0:
                pl.when(jnp.logical_not((l_ == zl) & (core == zl)))(arrival.wait_recv)
            else:
                arrival.wait_recv()

    total = s3_r[0].astype(F32)
    for z_ in range(1, 4 * nl):
        total = total + s3_r[z_].astype(F32)
    gh_out[:, 0:LANES] = total[:per_y, 0:LANES]
    gh_out[:, LANES:lead] = total[per_y:, 0:LANES]
    gh_out[:, lead:depth] = total[:per_y, LANES : LANES + depth - lead]
    second = total[per_y:, LANES : 2 * LANES]
    lane = lax.broadcasted_iota(jnp.int32, second.shape, 1)
    tail = jnp.where((lane >= MAIN) & (lane < MAIN + EXTRA), second, 0.0)
    folded = tail
    for b in range(1, GROUPS):
        folded = folded + pltpu.roll(tail, LANES - 4 * b, 1)
    go_out[...] = jnp.where(lane < MAIN, second, folded)[:, : go_out.shape[1]]
    last_left()


def flush(gh_in, go_in, gm_in, gh_out, go_out, gm_out, sem):
    copies = [pltpu.make_async_copy(a, b, sem.at[i]) for i, (a, b) in enumerate(((gm_in, gm_out), (gh_in, gh_out), (go_in, go_out)))]
    for copy in copies:
        copy.start()
    for copy in copies:
        copy.wait()


def solution(mesh, dims=(4, 2, 8)):
    def local(mesh_latent, grid_latent, edge_sources, edge_weights, area_weight, band_counts, target, hidden_weight, out_weight):
        nx, nl, ny = dims
        _, depth, nodes = mesh_latent.shape
        points = grid_latent.shape[2]
        variables = target.shape[0]
        per_x, per_z, per_y = depth // nx, depth // (nx * nl), depth // (nx * nl * ny)
        width, lead = depth + LANES, 2 * LANES
        tall = width - lead
        area = area_weight.reshape(1, points)
        vm, dma = pltpu.VMEM, pltpu.SemaphoreType.DMA
        scratch = [
            vm((depth, nodes), BF16), vm((depth, points), BF16), vm((3, points), jnp.int32), vm((3, points), BF16),
            vm((1, points), F32), vm((1, 1), jnp.int32), vm((variables, points), BF16), vm((depth, depth), BF16), vm((variables, depth), BF16),
            vm((104, points), F32), vm((1, points), F32), vm((depth, depth), BF16), vm((LANES, depth), F32), vm((depth, LANES), BF16), vm((LANES, depth), BF16),
            vm((depth, 2 * HALO), BF16), vm((depth, 2 * HALO), BF16), vm((depth, points), F32), vm((depth, points), F32),
            vm((nodes + 2 * HALO, points), BF16), vm((depth, points), BF16), vm((depth, points), BF16), vm((depth, points), F32),
            vm((2, depth // 2, LANES), BF16), vm((2, depth // 2, LANES), BF16), vm((2, depth // 2, LANES), BF16), vm((2, depth // 2, LANES), BF16),
            vm((CHUNKS, BLOCKS, MAIN, LANES), BF16), vm((2, EXTRA, LANES), BF16), vm((2, 8, ROWS, LANES), BF16), vm((8, EXTRA, LANES), BF16),
            vm((2, 8, ROWS + EXTRA, LANES), BF16), vm((CHUNKS, 4, ROWS + EXTRA, LANES), BF16),
            vm((depth, width), F32), vm((depth, nodes), F32), vm((depth, points), BF16), vm((depth, points), BF16), vm((LANES, points), BF16),
            vm((nx, per_z, tall), BF16), vm((nx, per_z, tall), BF16), vm((nx, per_z, lead), BF16), vm((nx, per_z, lead), BF16),
            vm((nx, per_z, tall), F32), vm((nx, per_z, tall), BF16), vm((nx - 1, per_z, tall), BF16),
            vm((ny, nx * per_y, lead), F32), vm((ny, nx * per_y, lead), BF16), vm((ny - 1, nx * per_y, lead), BF16),
            vm((ny, 2 * per_y, lead), F32), vm((ny, 2 * per_y, lead), BF16), vm((ny - 1, 2 * per_y, lead), BF16),
            vm((nx, 2 * per_y, LANES), F32), vm((nx, 2 * per_y, LANES), BF16), vm((nx - 1, 2 * per_y, LANES), BF16),
            vm((2 * per_y, 3 * LANES), BF16), vm((4 * nl, 2 * per_y, 3 * LANES), BF16),
            pltpu.SemaphoreType.REGULAR((3,)),
            vm((1, points), F32), vm((2, EXTRA, LANES), BF16), vm((2, EXTRA, LANES), BF16), vm((2, ROWS, LANES), BF16), dma((2, 4)),
            dma((9,)), dma((2, 2)), dma((2, 2)), dma((CHUNKS, 4)), dma((2, 8)), dma((2,)), dma((8,)),
            dma((2, 8)), dma((CHUNKS, 4)),
            dma((2, 2)), dma((2, nx - 1)), dma((2, ny - 1)), dma((2, ny - 1)), dma((2, nx - 1)), dma((8,)), dma((4 * nl,)),
        ]
        sums = pl.pallas_call(
            functools.partial(kernel, dims),
            out_shape=(
                pltpu.VMEM((per_y, depth), F32),
                pltpu.VMEM((per_y, variables), F32),
                pltpu.VMEM((1, depth, nodes), F32),
            ),
            in_specs=[pl.BlockSpec(memory_space=pl.ANY)] * 9,
            out_specs=[pl.BlockSpec(memory_space=pltpu.VMEM)] * 3,
            scratch_shapes=scratch,
            compiler_params=pltpu.CompilerParams(
                collective_id=0, has_side_effects=True, vmem_limit_bytes=62 * 1024 * 1024
            ),
            name="step",
        )(mesh_latent, grid_latent, edge_sources, edge_weights, area, band_counts.reshape(1, 1), target, hidden_weight, out_weight.T)
        return pl.pallas_call(
            flush,
            out_shape=tuple(jax.ShapeDtypeStruct(a.shape, F32) for a in sums),
            in_specs=[pl.BlockSpec(memory_space=pl.ANY)] * 3,
            out_specs=[pl.BlockSpec(memory_space=pl.ANY)] * 3,
            scratch_shapes=[dma((3,))],
            compiler_params=pltpu.CompilerParams(vmem_limit_bytes=1024 * 1024),
            name="flush",
        )(*sums)

    return jax.shard_map(
        local,
        mesh=mesh,
        in_specs=(
            P("member", None, "grid"),
            P("member", None, "grid"),
            P(None, "grid"),
            P(None, "grid"),
            P("grid"),
            P("grid"),
            P(None, "grid"),
            P(),
            P(),
        ),
        out_specs=(P("grid", None), P("grid", None), P("member", None, "grid")),
        check_vma=False,
    )
```

```python
import functools

import jax
import jax.numpy as jnp
from jax import lax
from jax.experimental import pallas as pl
from jax.experimental.pallas import tpu as pltpu
from jax.sharding import PartitionSpec as P

HALO = 64
LANES = 128
CHUNKS = 4
BLOCKS = 2
GROUPS = 4
KEEPERS = (4, 6)
ROWS = 48
MAIN = 96
EXTRA = 16
MESH = pl.DeviceIdType.MESH

smooth_sq = 0.01
loss_scale = 4096.0

F32 = jnp.float32
BF16 = jnp.bfloat16


def slope(diff):
    return diff * lax.rsqrt(diff * diff + smooth_sq)


def dot(a, b, da, db):
    return lax.dot_general(a, b, (((da,), (db,)), ((), ())), preferred_element_type=F32)


def low_lanes(shape):
    return lax.broadcasted_iota(jnp.int32, shape, 1) < HALO


def pack(tile):
    half = tile.shape[0] // 2
    top, bottom = tile[:half], tile[half:]
    low = low_lanes(top.shape)
    down = jnp.where(low, top, pltpu.roll(bottom, HALO, 1))
    up = jnp.where(low, pltpu.roll(top, HALO, 1), bottom)
    return down, up


def unpack(below, above):
    low = low_lanes(below.shape)
    top = jnp.where(low, below, pltpu.roll(above, HALO, 1))
    bottom = jnp.where(low, pltpu.roll(below, HALO, 1), above)
    return top, bottom


def kernel(
    dims,
    mesh_in, grid_in, src_in, wgt_in, area_in, count_in, target_in, hw_in, ow_in,
    gh_out, go_out, gm_out,
    mesh_v, grid_v, src_v, wgt_v, area_v, count_v, tgt_v, hw_v, ow_v,
    tgt_f, coef_v, hw_t, ow_f, ow_r, ow_t, halo_v, hh_v, xo_v, po_v, adj_v, x_v, h_v, f_v,
    halo_s, halo_r, ghalo_s, ghalo_r,
    pred_s, pext_s, pred_r, pext_r, grad_s, grad_r,
    gw_v, eg_v, dpre_v, dx_v, gp_v, a0_s, a0_r, b0_s, b0_r, a1_f, a1_s, a1_r, b1_f, b1_s, b1_r, a2_f, a2_s, a2_r, b2_f, b2_s, b2_r, s3_s, s3_r,
    near_sem, coef_r, ttail_s, ttail_r, tgt_r, t_sem, load_sem, halo_sem, ghalo_sem, p_send, p_recv, pe_send, pe_recv, g_send, g_recv,
    s0_sem, a1_sem, b1_sem, a2_sem, b2_sem, s3_send, s3_recv,
):
    nx, nl, ny = dims
    nodes = mesh_v.shape[1]
    depth = hw_v.shape[0]
    width = depth + LANES
    points = grid_v.shape[1] // CHUNKS
    member, band = lax.axis_index("member"), lax.axis_index("grid")
    zh, core = member // 2, member % 2
    xi, zl, yi = band // (nl * ny), (band // ny) % nl, band % ny
    bands = nx * nl * ny

    def at(zh_=None, core_=None, x_=None, zl_=None, y_=None):
        zh_ = zh if zh_ is None else zh_
        core_ = core if core_ is None else core_
        x_ = xi if x_ is None else x_
        zl_ = zl if zl_ is None else zl_
        y_ = yi if y_ is None else y_
        return (zh_ * 2 + core_, x_ * (nl * ny) + zl_ * ny + y_)

    above = (member, (band + 1) % bands)
    below = (member, (band + bands - 1) % bands)

    def remote(src, dst, sems, i, device):
        return pltpu.make_async_remote_copy(
            src_ref=src, dst_ref=dst, send_sem=sems.at[0, i], recv_sem=sems.at[1, i],
            device_id=device, device_id_type=MESH,
        )

    barrier = pltpu.get_barrier_semaphore()
    other = xi * (nl * ny) + (1 - zl) * ny + yi
    column = [(a, b, c) for a in (2, 1, 3, 0) for b in range(2) for c in range(nl) if (a, b, c) != (0, 0, 0)]
    beside = [at(y_=(yi + 1) % ny), at(y_=(yi + ny - 1) % ny), at(x_=(xi + 1) % nx), at(x_=(xi + nx - 1) % nx)]
    partners = [above, below] + beside
    partners += [at(zh_=(zh + a) % 4, core_=(core + b) % 2, zl_=(zl + c) % nl) for a, b, c in column]

    def tell(i):
        for partner in beside if i == 0 else beside[:2]:
            pl.semaphore_signal(near_sem.at[i], inc=1, device_id=partner, device_id_type=MESH)

    def hear(i):
        pl.semaphore_wait(near_sem.at[i], 4 if i == 0 else 2)

    def load(i, src, dst):
        copy = pltpu.make_async_copy(src, dst, load_sem.at[i])
        copy.start()
        return copy

    load_mesh = load(0, mesh_in.at[0], mesh_v)
    for partner in partners:
        pl.semaphore_signal(barrier, inc=1, device_id=partner, device_id_type=MESH)
    load_src = load(1, src_in, src_v)
    load_wgt = load(2, wgt_in, wgt_v)
    load_hw = load(3, hw_in, hw_v)
    load_ow = load(4, ow_in, ow_v)
    load_grid = load(5, grid_in.at[0], grid_v)
    load_area = load(6, area_in, area_v)
    load_tgt = load(7, target_in, tgt_v)
    load_count = load(8, count_in, count_v)

    load_mesh.wait()
    down, up = pack(mesh_v[...].astype(F32))
    halo_s[0] = down.astype(BF16)
    halo_s[1] = up.astype(BF16)
    pl.semaphore_wait(barrier, len(partners))
    halo_down = remote(halo_s.at[0], halo_r.at[0], halo_sem, 0, below)
    halo_up = remote(halo_s.at[1], halo_r.at[1], halo_sem, 1, above)
    halo_down.start()
    halo_up.start()
    tell(0)


    load_hw.wait()
    hw_t[...] = hw_v[...].astype(F32).T.astype(BF16)
    load_ow.wait()
    count = ow_v.shape[0]
    ow_f[MAIN:LANES] = jnp.zeros((LANES - MAIN, depth), F32)
    ow_f[0:count] = ow_v[...].astype(F32)
    tail = ow_f[MAIN : MAIN + 8]
    tail = tail + pltpu.roll(tail, 4, 0)
    ow_f[MAIN : MAIN + 8] = tail
    ow_f[MAIN + 8 : MAIN + 16] = tail
    ow_t[...] = ow_f[...].astype(BF16)
    ow_r[...] = ow_f[...].T.astype(BF16)

    load_src.wait()
    load_wgt.wait()
    row = lax.broadcasted_iota(jnp.int32, (nodes + 2 * HALO, points), 0)
    slot = jnp.where(row < nodes, row, jnp.where(row < nodes + HALO, row - (nodes + HALO), row - HALO))
    for chunk in range(CHUNKS):
        cols = pl.ds(chunk * points, points)
        adj = jnp.zeros(row.shape, F32)
        for k in range(3):
            source = src_v[pl.ds(k, 1), cols] - band * nodes
            weight = wgt_v[:, cols].astype(F32)[k : k + 1]
            adj = jnp.where(source == slot, weight, adj)
        adj_v[:, cols] = adj.astype(BF16)

    load_tgt.wait()
    tgt_f[0 : tgt_v.shape[0]] = tgt_v[...].astype(F32)
    load_area.wait()
    load_count.wait()
    place = lax.broadcasted_iota(jnp.int32, (1, CHUNKS * points), 1)
    live = (place < count_v[...]).astype(F32)
    coef_v[...] = loss_scale * area_v[...] * live / tgt_v.shape[0]
    group = lax.broadcasted_iota(jnp.int32, (EXTRA, LANES), 0) // 4

    def spread(blocks):
        out = blocks[0]
        for b in range(1, GROUPS):
            out = jnp.where(group == b, blocks[b], out)
        return out

    def rows_of(z_):
        return pl.ds(pl.multiple_of(ROWS * (z_ // 2), 16), ROWS)

    row8 = lax.broadcasted_iota(jnp.int32, (8, LANES), 0)
    for sc in range(2):
        targets = []
        for b in range(GROUPS):
            tail = tgt_f[MAIN : MAIN + 8, pl.ds((sc * GROUPS + b) * LANES, LANES)]
            tail = jnp.where(row8 < 4, tail, pltpu.roll(tail, 4, 0))
            targets.append(jnp.concatenate([tail, tail], axis=0))
        ttail_s[sc] = spread(targets).astype(BF16)
    mate = at(zl_=1 - zl)
    lent = [remote(coef_v, coef_r, t_sem, 0, mate), remote(ttail_s, ttail_r, t_sem, 1, mate)]
    for i in range(2):
        lanes = pl.ds(pl.multiple_of((2 * i + core) * points + (zh % 2) * LANES, LANES), LANES)
        lent.append(remote(tgt_v.at[rows_of(zh), lanes], tgt_r.at[i], t_sem, 2 + i, mate))
    for copy in lent:
        copy.start()

    turn = 1 + (ny - 2) * core
    sent = []

    def halos_left():
        halo_down.wait_send()
        halo_up.wait_send()

    def points_left():
        for k in range(CHUNKS):
            for z_ in range(4):
                pred_copy(k, z_).wait_send()
            pl.when(core == k % 2)(functools.partial(left_grad, k))
        for sc in range(2):
            pext_copy(sc).wait_send()

    def sent_left():
        for copy in sent:
            copy.wait_send()
        sent.clear()

    def last_left():
        for a in range(4):
            for c_ in range(2):
                left = s3_copy((zh + a) % 4, c_, here)
                if a == 0:
                    pl.when(jnp.logical_not((zl == core) & (core == c_)))(left.wait_send)
                else:
                    left.wait_send()

    def left_grad(k):
        def left(rows):
            for j in range(8):
                grad_copy(k, j, rows).wait_send()

        if k % 2 == 0:
            pl.when(member == KEEPERS[k // 2])(functools.partial(left, ROWS + EXTRA))
            pl.when(member != KEEPERS[k // 2])(functools.partial(left, ROWS))
        else:
            left(ROWS)

    load_grid.wait()
    for half in range(2):
        cols = pl.ds(half * 2 * points, 2 * points)
        xo_v[:, cols] = dot(mesh_v[...], adj_v[0:nodes, cols], 1, 0) + grid_v[:, cols].astype(F32)
        po_v[:, cols] = dot(hw_t[...], xo_v[:, cols].astype(BF16), 1, 0)
    halo_down.wait_recv()
    halo_up.wait_recv()
    top, bottom = unpack(halo_r[1].astype(F32), halo_r[0].astype(F32))
    halo_v[0 : depth // 2] = top.astype(BF16)
    halo_v[depth // 2 : depth] = bottom.astype(BF16)
    hh_v[...] = dot(hw_t[...], halo_v[...], 1, 0).astype(BF16)

    def toward(o):
        return (zh + zl + o + core * (3 - 2 * o)) % 4

    def pred_copy(k, z_):
        return pltpu.make_async_remote_copy(
            src_ref=pred_s.at[k, z_ % 2, rows_of(z_)], dst_ref=pred_r.at[k // 2, member],
            send_sem=p_send.at[k, z_], recv_sem=p_recv.at[k // 2, member],
            device_id=at(zh_=z_, core_=k % 2, zl_=1 - zl), device_id_type=MESH,
        )

    def pred_arrival(k, j):
        return pltpu.make_async_remote_copy(
            src_ref=pred_s.at[k, 0, pl.ds(0, ROWS)], dst_ref=pred_r.at[k // 2, j],
            send_sem=p_send.at[k, 0], recv_sem=p_recv.at[k // 2, j],
            device_id=(j, other), device_id_type=MESH,
        )

    def grad_copy(k, j, rows):
        return pltpu.make_async_remote_copy(
            src_ref=grad_s.at[k // 2, j, pl.ds(0, rows)], dst_ref=grad_r.at[k, zh, pl.ds(0, rows)],
            send_sem=g_send.at[k // 2, j], recv_sem=g_recv.at[k, zh],
            device_id=(j, other), device_id_type=MESH,
        )

    def grad_arrival(k, z_):
        rows = ROWS + EXTRA if 2 * z_ + k % 2 == KEEPERS[k // 2] else ROWS
        return pltpu.make_async_remote_copy(
            src_ref=grad_s.at[0, 0, pl.ds(0, rows)], dst_ref=grad_r.at[k, z_, pl.ds(0, rows)],
            send_sem=g_send.at[0, 0], recv_sem=g_recv.at[k, z_],
            device_id=at(zh_=z_, core_=k % 2, zl_=1 - zl), device_id_type=MESH,
        )

    def pext_copy(sc):
        return pltpu.make_async_remote_copy(
            src_ref=pext_s.at[sc], dst_ref=pext_r.at[member],
            send_sem=pe_send.at[sc], recv_sem=pe_recv.at[member],
            device_id=(KEEPERS[sc], other), device_id_type=MESH,
        )

    def pext_arrival(sc, j):
        return pltpu.make_async_remote_copy(
            src_ref=pext_s.at[sc], dst_ref=pext_r.at[j],
            send_sem=pe_send.at[sc], recv_sem=pe_recv.at[j],
            device_id=(j, other), device_id_type=MESH,
        )

    def forward(sc):
        cols = pl.ds(sc * 2 * points, 2 * points)
        pre = po_v[:, cols] + dot(hh_v[...], adj_v[nodes : nodes + 2 * HALO, cols], 1, 0)
        sig = 0.5 * jnp.tanh(0.5 * pre) + 0.5
        h_v[:, cols] = (pre * sig).astype(BF16)
        f_v[:, cols] = sig * (1.0 + pre * (1.0 - sig))
        pred = dot(ow_t[...], h_v[:, cols], 1, 0)
        tails = []
        for b in range(GROUPS):
            block = pred[:, b * LANES : (b + 1) * LANES]
            pred_s[2 * sc + b // BLOCKS, b % BLOCKS] = block[:MAIN].astype(BF16)
            tails.append(block[MAIN : MAIN + EXTRA])
        pext_s[sc] = spread(tails).astype(BF16)
        for k in (2 * sc, 2 * sc + 1):
            for o in (1, 2, 0, 3):
                pred_copy(k, toward(o)).start()
        pext_copy(sc).start()

    def fair(preds, target, weight):
        out = [slope(p - target) * (1.0 / 8.0) for p in preds]
        pairs = [jnp.zeros(target.shape, F32) for _ in preds]
        for i in range(8):
            for j in range(i + 1, 8):
                s = slope(preds[i] - preds[j])
                pairs[i] = pairs[i] + s
                pairs[j] = pairs[j] - s
        return [weight * (o - q * (1.0 / 56.0)) for o, q in zip(out, pairs)]

    def pair_up(k):
        @pl.when(core == k % 2)
        def _():
            for j in range(8):
                pred_arrival(k, j).wait_recv()
            weight = coef_r[:, pl.ds(pl.multiple_of(k * points + (zh % 2) * LANES, LANES), LANES)]

            def tile(t, _):
                rows = pl.ds(pl.multiple_of(t * 16, 16), 16)
                target = tgt_r[k // 2, rows].astype(F32)
                grads = fair([pred_r[k // 2, j, rows].astype(F32) for j in range(8)], target, weight)
                for j in range(8):
                    grad_s[k // 2, j, rows] = grads[j].astype(BF16)
                return 0

            lax.fori_loop(0, ROWS // 16, tile, 0)
            def send(rows):
                for o in (1, 2, 0, 3):
                    for c_ in range(2):
                        grad_copy(k, toward(o) * 2 + c_, rows).start()

            if k % 2 == 0:
                keeper = KEEPERS[k // 2]

                @pl.when(member == keeper)
                def _():
                    pair_up_tail(k // 2)
                    send(ROWS + EXTRA)

                pl.when(member != keeper)(functools.partial(send, ROWS))
            else:
                send(ROWS)

    def pair_up_tail(sc):
        for j in range(8):
            pext_arrival(sc, j).wait_recv()
        weights = []
        for b in range(GROUPS):
            at_b = pl.ds((sc * GROUPS + b) * LANES, LANES)
            weights.append(jnp.broadcast_to(coef_r[:, at_b], (EXTRA, LANES)))
        grads = fair([pext_r[j].astype(F32) for j in range(8)], ttail_r[sc].astype(F32), spread(weights))
        for j in range(8):
            grad_s[sc, j, ROWS : ROWS + EXTRA] = grads[j].astype(BF16)

    def backward(sc):
        cols = pl.ds(sc * 2 * points, 2 * points)
        for k in (2 * sc, 2 * sc + 1):
            for z_ in range(4):
                grad_arrival(k, z_).wait_recv()

        tail = grad_r[2 * sc, KEEPERS[sc] // 2, ROWS : ROWS + EXTRA].astype(F32)
        blocks = []
        for b in range(GROUPS):
            mine = jnp.where(group == b, tail, 0.0).astype(BF16)
            main = [grad_r[2 * sc + b // BLOCKS, b % BLOCKS + 2 * i, 0:ROWS] for i in range(2)]
            blocks.append(jnp.concatenate([*main, mine, jnp.zeros((LANES - MAIN - EXTRA, LANES), BF16)], axis=0))
        gpred = jnp.concatenate(blocks, axis=1)
        dh = dot(ow_r[...], gpred, 1, 0)
        dpre_v[:, cols] = (dh * f_v[:, cols]).astype(BF16)
        gp_v[:, cols] = gpred

    forward(0)
    hear(0)
    tell(1)
    forward(1)
    for half in range(2):
        cols = pl.ds(half * 2 * points, 2 * points)
        x_v[:, cols] = (xo_v[:, cols] + dot(halo_v[...], adj_v[nodes : nodes + 2 * HALO, cols], 1, 0)).astype(BF16)
    for copy in lent:
        copy.wait_recv()
    sent.extend(lent)
    hear(1)
    tell(2)
    for k in range(CHUNKS):
        pair_up(k)
    lead = 2 * LANES
    per_x, per_z, per_y = depth // nx, depth // (nx * nl), depth // (nx * nl * ny)

    def part(x_, core_):
        return pl.ds(pl.multiple_of(x_ * per_x + core_ * per_z, 8), per_z)

    hear(2)
    backward(0)
    early, late = pl.ds(0, 2 * points), pl.ds(2 * points, 2 * points)
    gw_v[:, 0:depth] = dot(x_v[:, early], dpre_v[:, early], 1, 1)
    gw_v[:, depth:width] = dot(h_v[:, early], gp_v[:, early], 1, 1)
    backward(1)
    gw_v[:, 0:lead] += dot(x_v[:, late], dpre_v[0:lead, late], 1, 1)
    for x_ in range(nx):
        b0_s[x_] = gw_v[part(x_, 1 - core), 0:lead].astype(BF16)
    b0 = remote(b0_s, b0_r, s0_sem, 0, at(core_=1 - core))
    b0.start()
    gw_v[:, lead:depth] += dot(x_v[:, late], dpre_v[lead:depth, late], 1, 1)
    gw_v[:, depth:width] += dot(h_v[:, late], gp_v[:, late], 1, 1)
    for x_ in range(nx):
        a0_s[x_] = gw_v[part(x_, 1 - core), lead:width].astype(BF16)
    a0 = remote(a0_s, a0_r, s0_sem, 1, at(core_=1 - core))
    a0.start()
    sent.extend([b0, a0])

    b0.wait_recv()
    for x_ in range(nx):
        total = gw_v[part(x_, core), 0:lead] + b0_r[x_].astype(F32)
        for y_ in range(ny):
            b1_f[y_, x_ * per_y : (x_ + 1) * per_y] = total[y_ * per_y : (y_ + 1) * per_y]
    b1 = []
    for s in (4, 3, 5, 2, 6, 1, 7):
        if s < ny:
            y_ = (yi + s * turn) % ny
            b1_s[y_] = b1_f[y_].astype(BF16)
            copy = remote(b1_s.at[y_], b1_r.at[s - 1], b1_sem, s - 1, at(y_=y_))
            copy.start()
            b1.append(copy)
    a0.wait_recv()
    for x_ in range(nx):
        a1_f[x_] = gw_v[part(x_, core), lead:width] + a0_r[x_].astype(F32)
    a1 = []
    for s in (2, 1, 3):
        if s < nx:
            x_ = (xi + s * (1 + (nx - 2) * core)) % nx
            a1_s[x_] = a1_f[x_].astype(BF16)
            copy = remote(a1_s.at[x_], a1_r.at[s - 1], a1_sem, s - 1, at(x_=x_))
            copy.start()
            a1.append(copy)
    sent.extend(a1 + b1)

    for half in range(2):
        cols = pl.ds(half * 2 * points, 2 * points)
        dx_v[:, cols] = dot(hw_v[...], dpre_v[:, cols], 1, 0).astype(BF16)
    down, up = pack(dot(dx_v[...], adj_v[nodes : nodes + 2 * HALO], 1, 1))
    ghalo_s[0] = down.astype(BF16)
    ghalo_s[1] = up.astype(BF16)
    ghalo_down = remote(ghalo_s.at[0], ghalo_r.at[0], ghalo_sem, 0, below)
    ghalo_up = remote(ghalo_s.at[1], ghalo_r.at[1], ghalo_sem, 1, above)
    ghalo_down.start()
    ghalo_up.start()
    sent.extend([ghalo_down, ghalo_up])
    eg_v[...] = dot(dx_v[...], adj_v[0:nodes], 1, 1)
    halos_left()
    points_left()

    for copy in a1:
        copy.wait_recv()
    total = a1_f[xi]
    for s in range(nx - 1):
        total = total + a1_r[s].astype(F32)
    for y_ in range(ny):
        rows = total[y_ * per_y : (y_ + 1) * per_y]
        rest = jnp.concatenate([rows[:, lead:], jnp.zeros((per_y, LANES), F32)], axis=1)
        a2_f[y_] = jnp.concatenate([rows[:, :lead], rest], axis=0)
        a2_s[y_] = a2_f[y_].astype(BF16)
    a2 = []
    for s in (4, 3, 5, 2, 6, 1, 7):
        if s < ny:
            y_ = (yi + s * turn) % ny
            copy = remote(a2_s.at[y_], a2_r.at[s - 1], a2_sem, s - 1, at(y_=y_))
            copy.start()
            a2.append(copy)
    for copy in b1:
        copy.wait_recv()
    total = b1_f[yi]
    for s in range(ny - 1):
        total = total + b1_r[s].astype(F32)
    for x_ in range(nx):
        rows = total[x_ * per_y : (x_ + 1) * per_y]
        b2_f[x_] = jnp.concatenate([rows[:, :LANES], rows[:, LANES:]], axis=0)
        b2_s[x_] = b2_f[x_].astype(BF16)
    b2 = []
    for s in (2, 1, 3):
        if s < nx:
            x_ = (xi + s * (1 + (nx - 2) * core)) % nx
            copy = remote(b2_s.at[x_], b2_r.at[s - 1], b2_sem, s - 1, at(x_=x_))
            copy.start()
            b2.append(copy)
    sent_left()
    sent.extend(a2 + b2)

    ghalo_down.wait_recv()
    ghalo_up.wait_recv()
    top, bottom = unpack(ghalo_r[1].astype(F32), ghalo_r[0].astype(F32))
    gm_out[0, 0 : depth // 2] = eg_v[0 : depth // 2] + top
    gm_out[0, depth // 2 : depth] = eg_v[depth // 2 : depth] + bottom

    for copy in b2:
        copy.wait_recv()
    total = b2_f[xi]
    for s in range(nx - 1):
        total = total + b2_r[s].astype(F32)
    s3_s[:, 0:LANES] = total.astype(BF16)
    for copy in a2:
        copy.wait_recv()
    total = a2_f[yi]
    for s in range(ny - 1):
        total = total + a2_r[s].astype(F32)
    s3_s[:, LANES : 3 * LANES] = total.astype(BF16)
    here = zh * nl + zl

    def s3_copy(z_, c_, slot):
        return pltpu.make_async_remote_copy(
            src_ref=s3_s, dst_ref=s3_r.at[slot],
            send_sem=s3_send.at[z_ * 2 + c_], recv_sem=s3_recv.at[slot],
            device_id=at(zh_=z_, core_=c_, zl_=core), device_id_type=MESH,
        )

    for z_ in range(4):
        for c_ in range(2):
            mine = (zh == z_) & (zl == core) & (core == c_)
            pl.when(jnp.logical_not(mine))(s3_copy(z_, c_, here).start)

            @pl.when(mine)
            def _():
                s3_r[here] = s3_s[...]

    sent_left()
    for a in range(4):
        for l_ in range(nl):
            arrival = s3_copy(0, 0, (zh + a) % 4 * nl + l_)
            if a == 0:
                pl.when(jnp.logical_not((l_ == zl) & (core == zl)))(arrival.wait_recv)
            else:
                arrival.wait_recv()

    total = s3_r[0].astype(F32)
    for z_ in range(1, 4 * nl):
        total = total + s3_r[z_].astype(F32)
    gh_out[:, 0:LANES] = total[:per_y, 0:LANES]
    gh_out[:, LANES:lead] = total[per_y:, 0:LANES]
    gh_out[:, lead:depth] = total[:per_y, LANES : LANES + depth - lead]
    second = total[per_y:, LANES : 2 * LANES]
    lane = lax.broadcasted_iota(jnp.int32, second.shape, 1)
    tail = jnp.where((lane >= MAIN) & (lane < MAIN + EXTRA), second, 0.0)
    folded = tail
    for b in range(1, GROUPS):
        folded = folded + pltpu.roll(tail, LANES - 4 * b, 1)
    go_out[...] = jnp.where(lane < MAIN, second, folded)[:, : go_out.shape[1]]
    last_left()


def flush(gh_in, go_in, gm_in, gh_out, go_out, gm_out, sem):
    copies = [pltpu.make_async_copy(a, b, sem.at[i]) for i, (a, b) in enumerate(((gm_in, gm_out), (gh_in, gh_out), (go_in, go_out)))]
    for copy in copies:
        copy.start()
    for copy in copies:
        copy.wait()


def solution(mesh, dims=(4, 2, 8)):
    def local(mesh_latent, grid_latent, edge_sources, edge_weights, area_weight, band_counts, target, hidden_weight, out_weight):
        nx, nl, ny = dims
        _, depth, nodes = mesh_latent.shape
        points = grid_latent.shape[2]
        variables = target.shape[0]
        per_x, per_z, per_y = depth // nx, depth // (nx * nl), depth // (nx * nl * ny)
        width, lead = depth + LANES, 2 * LANES
        tall = width - lead
        area = area_weight.reshape(1, points)
        vm, dma = pltpu.VMEM, pltpu.SemaphoreType.DMA
        scratch = [
            vm((depth, nodes), BF16), vm((depth, points), BF16), vm((3, points), jnp.int32), vm((3, points), BF16),
            vm((1, points), F32), vm((1, 1), jnp.int32), vm((variables, points), BF16), vm((depth, depth), BF16), vm((variables, depth), BF16),
            vm((104, points), F32), vm((1, points), F32), vm((depth, depth), BF16), vm((LANES, depth), F32), vm((depth, LANES), BF16), vm((LANES, depth), BF16),
            vm((depth, 2 * HALO), BF16), vm((depth, 2 * HALO), BF16), vm((depth, points), F32), vm((depth, points), F32),
            vm((nodes + 2 * HALO, points), BF16), vm((depth, points), BF16), vm((depth, points), BF16), vm((depth, points), F32),
            vm((2, depth // 2, LANES), BF16), vm((2, depth // 2, LANES), BF16), vm((2, depth // 2, LANES), BF16), vm((2, depth // 2, LANES), BF16),
            vm((CHUNKS, BLOCKS, MAIN, LANES), BF16), vm((2, EXTRA, LANES), BF16), vm((2, 8, ROWS, LANES), BF16), vm((8, EXTRA, LANES), BF16),
            vm((2, 8, ROWS + EXTRA, LANES), BF16), vm((CHUNKS, 4, ROWS + EXTRA, LANES), BF16),
            vm((depth, width), F32), vm((depth, nodes), F32), vm((depth, points), BF16), vm((depth, points), BF16), vm((LANES, points), BF16),
            vm((nx, per_z, tall), BF16), vm((nx, per_z, tall), BF16), vm((nx, per_z, lead), BF16), vm((nx, per_z, lead), BF16),
            vm((nx, per_z, tall), F32), vm((nx, per_z, tall), BF16), vm((nx - 1, per_z, tall), BF16),
            vm((ny, nx * per_y, lead), F32), vm((ny, nx * per_y, lead), BF16), vm((ny - 1, nx * per_y, lead), BF16),
            vm((ny, 2 * per_y, lead), F32), vm((ny, 2 * per_y, lead), BF16), vm((ny - 1, 2 * per_y, lead), BF16),
            vm((nx, 2 * per_y, LANES), F32), vm((nx, 2 * per_y, LANES), BF16), vm((nx - 1, 2 * per_y, LANES), BF16),
            vm((2 * per_y, 3 * LANES), BF16), vm((4 * nl, 2 * per_y, 3 * LANES), BF16),
            pltpu.SemaphoreType.REGULAR((3,)),
            vm((1, points), F32), vm((2, EXTRA, LANES), BF16), vm((2, EXTRA, LANES), BF16), vm((2, ROWS, LANES), BF16), dma((2, 4)),
            dma((9,)), dma((2, 2)), dma((2, 2)), dma((CHUNKS, 4)), dma((2, 8)), dma((2,)), dma((8,)),
            dma((2, 8)), dma((CHUNKS, 4)),
            dma((2, 2)), dma((2, nx - 1)), dma((2, ny - 1)), dma((2, ny - 1)), dma((2, nx - 1)), dma((8,)), dma((4 * nl,)),
        ]
        sums = pl.pallas_call(
            functools.partial(kernel, dims),
            out_shape=(
                pltpu.VMEM((per_y, depth), F32),
                pltpu.VMEM((per_y, variables), F32),
                pltpu.VMEM((1, depth, nodes), F32),
            ),
            in_specs=[pl.BlockSpec(memory_space=pl.ANY)] * 9,
            out_specs=[pl.BlockSpec(memory_space=pltpu.VMEM)] * 3,
            scratch_shapes=scratch,
            compiler_params=pltpu.CompilerParams(
                collective_id=0, has_side_effects=True, vmem_limit_bytes=62 * 1024 * 1024
            ),
            name="step",
        )(mesh_latent, grid_latent, edge_sources, edge_weights, area, band_counts.reshape(1, 1), target, hidden_weight, out_weight.T)
        return pl.pallas_call(
            flush,
            out_shape=tuple(jax.ShapeDtypeStruct(a.shape, F32) for a in sums),
            in_specs=[pl.BlockSpec(memory_space=pl.ANY)] * 3,
            out_specs=[pl.BlockSpec(memory_space=pl.ANY)] * 3,
            scratch_shapes=[dma((3,))],
            compiler_params=pltpu.CompilerParams(vmem_limit_bytes=1024 * 1024),
            name="flush",
        )(*sums)

    return jax.shard_map(
        local,
        mesh=mesh,
        in_specs=(
            P("member", None, "grid"),
            P("member", None, "grid"),
            P(None, "grid"),
            P(None, "grid"),
            P("grid"),
            P("grid"),
            P(None, "grid"),
            P(),
            P(),
        ),
        out_specs=(P("grid", None), P("grid", None), P("member", None, "grid")),
        check_vma=False,
    )
```
